256 devices in a mesh: dp: 64 (over z, y, core), mp: 4 (over x).
Axes of the slice: x: 4, y: 4, z: 8, core: 2. Of those that a mesh axis runs over, the one named last changes fastest.
Arguments:
- grads: bfloat16 [64, 32, 512, 512], P('dp', None, None, 'mp'), may hold values from -600 to 600
- owner: int32 [32], replicated, may hold values from 0 to 63, as said below
Outputs:
- updates: bfloat16 [128, 512, 512], P('dp', None, 'mp')
The draws below stay inside these ranges and needn't reach their ends.
Inputs may be any that keep to these rules, and one draw needn't show every extreme that they name: `owner`: each entry is an index of dp. Each index of dp owns at most 2 blocks, and at least one owns exactly 2.
All inputs are finite; a program needn't handle non-finite values.
Results may differ from the reference program's by a relative error of at most 0.012.
The reference program's roundings to bfloat16 on the way (of `gradient` and `right_half`) count: a program that leaves them out, or rounds other values in their place, can miss the bound.
Values may be sent and summed in bfloat16 or wider, within the bound.
No kernel may reach another device: no remote copies, remote signals or barrier semaphores. Data moves between devices by JAX's collectives and lax.ppermute only.
A program may use at most 192 MiB of HBM per device.

```python
import math
import jax
import jax.numpy as jnp
from jax import lax

B = 512
ITERS = 3
MOST = 2
BLOCKS = 32
N_DP = 64


def log_scales(key, shape, top):
    return jnp.exp(jax.random.uniform(key, shape, minval=0.0, maxval=math.log(top)))


def draw_grads(key, part):
    key = jax.random.fold_in(key, 5)
    row_key, column_key, noise_key = jax.random.split(key, 3)
    row_scales = log_scales(row_key, (BLOCKS, B, 1), 10.0)
    column_scales = log_scales(column_key, (B,), 10.0)
    base = jax.random.truncated_normal(noise_key, -6.0, 6.0, (N_DP, BLOCKS, B, B))
    return (base * row_scales * column_scales).astype(jnp.bfloat16)


def draw_owner(key, part):
    key = jax.random.fold_in(key, 9)
    device_key, pick_key, order_key = jax.random.split(key, 3)
    inner = jax.random.permutation(device_key, N_DP - 2).astype(jnp.int32) + 1
    candidates = jnp.concatenate([jnp.array([0, N_DP - 1], dtype=jnp.int32), inner])
    pair_count = max(1, BLOCKS // 4)
    used_count = BLOCKS - pair_count
    chosen = candidates[:used_count][jax.random.permutation(pick_key, used_count)]
    listed = jnp.concatenate([jnp.repeat(chosen[:pair_count], 2), chosen[pair_count:]])
    ordering = jax.random.permutation(order_key, BLOCKS)
    return listed[ordering].astype(jnp.int32)


def setup_inputs(seed: int = 0) -> dict:
    streams_of = jax.random.split(jax.random.key(seed), 3)
    return {
        "grads": draw_grads(jax.random.fold_in(streams_of[2], 71), 0),
        "owner": draw_owner(jax.random.fold_in(streams_of[2], 71), 0),
    }


def inverse_root(statistic):
    extent = statistic.shape[0]
    identity = jnp.eye(extent, dtype=jnp.float32)
    scaling = 2.5 / jnp.sqrt(jnp.sum(statistic * statistic) + 1e-06)
    root_now = (scaling ** 0.25 * identity).astype(jnp.bfloat16)
    moment = (scaling * statistic).astype(jnp.bfloat16)
    for iteration in range(ITERS):
        factor = ((5.0 * identity - moment.astype(jnp.float32)) / 4.0).astype(jnp.bfloat16)
        root_now = jnp.dot(root_now, factor, preferred_element_type=jnp.float32).astype(jnp.bfloat16)
        square = jnp.dot(factor, factor, preferred_element_type=jnp.float32).astype(jnp.bfloat16)
        fourth = jnp.dot(square, square, preferred_element_type=jnp.float32).astype(jnp.bfloat16)
        moment = jnp.dot(fourth, moment, preferred_element_type=jnp.float32).astype(jnp.bfloat16)
    return root_now

def precondition(gradient_block):
    left_stat = jnp.dot(gradient_block, gradient_block.T, preferred_element_type=jnp.float32)
    right_stat = jnp.dot(gradient_block.T, gradient_block, preferred_element_type=jnp.float32)
    left_root = inverse_root(left_stat)
    right_root = inverse_root(right_stat)
    right_half = jnp.dot(gradient_block, right_root, preferred_element_type=jnp.float32).astype(jnp.bfloat16)
    return (math.sqrt(B) * jnp.dot(left_root, right_half, preferred_element_type=jnp.float32)).astype(jnp.bfloat16)

def reference(grads, owner):

    def accumulate(running, replica):
        return (running + replica.astype(jnp.float32), None)
    running, unused = lax.scan(accumulate, jnp.zeros(grads.shape[1:], jnp.float32), grads)
    gradient = (running / N_DP).astype(jnp.bfloat16)
    positions = jnp.arange(BLOCKS, dtype=jnp.int32)
    earlier = (owner[None, :] == owner[:, None]) & (positions[None, :] < positions[:, None])
    slot_of = (owner * MOST + lax.optimization_barrier(jnp.sum(earlier.astype(jnp.int32), axis=1))).astype(jnp.int32)
    blocks = lax.map(precondition, gradient)
    updates = jnp.zeros((N_DP * MOST, B, B), jnp.bfloat16).at[slot_of].set(blocks)
    return updates
```

```python
import math

import jax
import jax.numpy as jnp
from jax import lax
from jax.experimental import pallas as pl
from jax.experimental.pallas import tpu as pltpu
from jax.sharding import Mesh, PartitionSpec as P

ITERS = 3
MOST = 2
Z, Y, CORE = 8, 4, 2
DP = ("z", "y", "core")


def selection(target, slot_rank, capacity, devices):
    slot_index = jnp.arange(capacity * devices, dtype=jnp.int32)
    want_slot = slot_index // devices
    want_device = slot_index % devices
    matches = (slot_rank[None, :] == want_slot[:, None]) & (target[None, :] == want_device[:, None])
    return matches.astype(jnp.bfloat16)


def dot(a, b):
    return jnp.dot(a, b, preferred_element_type=jnp.float32)


def dot16(a, b):
    return dot(a, b).astype(jnp.bfloat16)


def precondition_kernel(p0, p1, p2, p3, out_ref):
    slots, extent, columns = out_ref.shape
    rows = lax.broadcasted_iota(jnp.int32, (extent, extent), 0)
    cols = lax.broadcasted_iota(jnp.int32, (extent, extent), 1)
    five = jnp.where(rows == cols, jnp.float32(5.0), jnp.float32(0.0))
    blocks, moments, scales = [], [], []
    for slot in range(slots):
        block = jnp.concatenate([p[slot] for p in (p0, p1, p2, p3)], axis=1)
        left = lax.dot_general(block, block, (((1,), (1,)), ((), ())), preferred_element_type=jnp.float32)
        right = lax.dot_general(block, block, (((0,), (0,)), ((), ())), preferred_element_type=jnp.float32)
        blocks.append(block)
        for stat in (left, right):
            total = jnp.sum(stat * stat, keepdims=True)
            scaling = 2.5 / jnp.sqrt(total + 1e-06)
            moments.append((scaling * stat).astype(jnp.bfloat16))
            scales.append(jnp.sqrt(jnp.sqrt(scaling)).astype(jnp.bfloat16).astype(jnp.float32))
    chains = range(2 * slots)
    roots = [None] * (2 * slots)
    for iteration in range(ITERS):
        factors = [((five - m.astype(jnp.float32)) * 0.25).astype(jnp.bfloat16) for m in moments]
        for c in chains:
            if iteration == 0:
                roots[c] = (scales[c] * factors[c].astype(jnp.float32)).astype(jnp.bfloat16)
            elif iteration == ITERS - 1 and c % 2 == 1:
                roots[c] = dot16(roots[c], factors[c][:, :columns])
            else:
                roots[c] = dot16(roots[c], factors[c])
        if iteration < ITERS - 1:
            squares = [dot16(f, f) for f in factors]
            fourths = [dot16(s, s) for s in squares]
            moments = [dot16(f, m) for f, m in zip(fourths, moments)]
    for slot in range(slots):
        right_half = dot16(blocks[slot], roots[2 * slot + 1])
        product = dot(roots[2 * slot], right_half)
        out_ref[slot] = (math.sqrt(extent) * product).astype(jnp.bfloat16)


def on_device(grads, owner):
    local_grads = grads[0]
    block_count, extent, columns = local_grads.shape
    devices = Z * Y * CORE
    half = extent // CORE
    positions = jnp.arange(block_count, dtype=jnp.int32)
    earlier = (owner[None, :] == owner[:, None]) & (positions[None, :] < positions[:, None])
    owner_rank = jnp.sum(earlier.astype(jnp.int32), axis=1)
    core = lax.axis_index("core")
    kept = lax.dynamic_slice_in_dim(local_grads, core * half, half, 1)
    sent = lax.dynamic_slice_in_dim(local_grads, (1 - core) * half, half, 1)
    arrived = lax.ppermute(sent, "core", [(0, 1), (1, 0)])
    pair = (kept.astype(jnp.float32) + arrived.astype(jnp.float32)).astype(jnp.bfloat16)
    pair = pair.reshape(block_count, Y, half // Y, columns)
    pieces = lax.all_to_all(pair, "y", split_axis=1, concat_axis=1, tiled=True)
    plane = jnp.sum(pieces.astype(jnp.float32), axis=1).astype(jnp.bfloat16)
    plane = plane.reshape(block_count, Z, half // (Y * Z), columns)
    pieces = lax.all_to_all(plane, "z", split_axis=1, concat_axis=1, tiled=True)
    summed = jnp.sum(pieces.astype(jnp.float32), axis=1)
    stripe = extent // devices
    mean_rows = (summed / devices).astype(jnp.bfloat16).reshape(block_count, stripe * columns)
    outgoing = jnp.dot(
        selection(owner, owner_rank, MOST, devices),
        mean_rows,
        preferred_element_type=jnp.float32,
    )
    outgoing = outgoing.astype(jnp.bfloat16).reshape(MOST, devices, stripe * columns)
    arrived = lax.all_to_all(outgoing, DP, split_axis=1, concat_axis=1, tiled=True)
    arrived = arrived.reshape(MOST, Z, Y, CORE, stripe, columns)
    owned = arrived.transpose(0, 3, 2, 1, 4, 5).reshape(MOST, extent, columns)
    bands = [owned]
    for shift in range(1, 4):
        bands.append(lax.ppermute(owned, "mp", [(i, (i + shift) % 4) for i in range(4)]))
    return pl.pallas_call(
        precondition_kernel,
        out_shape=jax.ShapeDtypeStruct(owned.shape, jnp.bfloat16),
        in_specs=[pl.BlockSpec(memory_space=pltpu.VMEM)] * 4,
        out_specs=pl.BlockSpec(memory_space=pltpu.VMEM),
        compiler_params=pltpu.CompilerParams(vmem_limit_bytes=48 * 1024 * 1024),
        name="precondition",
    )(*bands)


def solution(mesh):
    split = Mesh(mesh.devices.reshape(Z, Y, CORE, 4), ("z", "y", "core", "mp"))
    placed = (P(DP, None, None, "mp"), P())
    return jax.shard_map(
        on_device, mesh=split, in_specs=placed, out_specs=P(DP, None, "mp"), check_vma=False
    )
```

```python
import math

import jax
import jax.numpy as jnp
from jax import lax
from jax.experimental import pallas as pl
from jax.experimental.pallas import tpu as pltpu
from jax.sharding import Mesh, PartitionSpec as P

ITERS = 3
MOST = 2
Z, Y, CORE, MP = 8, 4, 2, 4
DP = ("z", "y", "core")
IN_VMEM = pl.BlockSpec(memory_space=pltpu.VMEM)
IN_SMEM = pl.BlockSpec(memory_space=pltpu.SMEM)
IN_HBM = pl.BlockSpec(memory_space=pltpu.HBM)
PARAMS = pltpu.CompilerParams(vmem_limit_bytes=12 * 1024 * 1024)
LARGE = pltpu.CompilerParams(vmem_limit_bytes=24 * 1024 * 1024)


def selection(owner, devices, stripe):
    blocks = owner.shape[0]
    positions = jnp.arange(blocks, dtype=jnp.int32)
    earlier = (owner[None, :] == owner[:, None]) & (positions[None, :] < positions[:, None])
    slot_of = owner * MOST + jnp.sum(earlier.astype(jnp.int32), axis=1)
    wanted = slot_of[:, None] * stripe + jnp.arange(stripe, dtype=jnp.int32)[None, :]
    row = jnp.arange(MOST * devices * stripe, dtype=jnp.int32)
    return (wanted.reshape(1, blocks * stripe) == row[:, None]).astype(jnp.bfloat16)


def dot(a, b):
    return jnp.dot(a, b, preferred_element_type=jnp.float32)


def dot16(a, b):
    return dot(a, b).astype(jnp.bfloat16)


def pieces_of(grads, core, y, shifts, name):
    blocks, extent, columns = grads.shape
    half = extent // CORE
    rows = half // Y
    cuts = 4
    group = blocks // cuts

    def kernel(core_ref, y_ref, in_ref, sent_ref, kept_ref, sems):
        copies = []
        for out_ref, which in ((sent_ref, 1 - core_ref[0]), (kept_ref, core_ref[0])):
            for i, shift in enumerate(shifts):
                first = pl.multiple_of(which * half + (y_ref[0] + shift) % Y * rows, rows)
                for cut in range(cuts):
                    some = pl.ds(cut * group, group)
                    source = in_ref.at[some, pl.ds(first, rows)]
                    copies.append(
                        pltpu.make_async_copy(source, out_ref.at[i, some], sems.at[len(copies)])
                    )
        for copy in copies:
            copy.start()
        for copy in copies:
            copy.wait()

    shape = pltpu.VMEM((len(shifts), blocks, rows, columns), grads.dtype)
    return pl.pallas_call(
        kernel,
        out_shape=(shape, shape),
        in_specs=[IN_SMEM, IN_SMEM, IN_HBM],
        out_specs=[IN_VMEM] * 2,
        scratch_shapes=[pltpu.SemaphoreType.DMA((2 * cuts * len(shifts),))],
        compiler_params=PARAMS,
        name=name,
    )(core, y, pltpu.with_memory_space_constraint(grads, pltpu.HBM))


def add_parts(parts, arrays, dtype, name):
    count = [entry[0][3] for entry in parts]
    rows, columns = arrays[0].shape[-2:]

    def kernel(*refs):
        ins, outs = refs[: len(arrays)], refs[len(arrays) :]
        for entry, out in zip(parts, outs):

            def add(b, carry):
                total = None
                for which, index, first, _ in entry:
                    value = ins[which][index, first + b].astype(jnp.float32)
                    total = value if total is None else total + value
                out[0, b] = total.astype(dtype)
                return carry

            lax.fori_loop(0, entry[0][3], add, 0, unroll=4)

    return pl.pallas_call(
        kernel,
        out_shape=[pltpu.VMEM((1, n, rows, columns), dtype) for n in count],
        in_specs=[IN_VMEM] * len(arrays),
        out_specs=[IN_VMEM] * len(parts),
        compiler_params=PARAMS,
        name=name,
    )(*arrays)


def plane_kernel(own_a_ref, own_b_ref, w_up_ref, w_down_ref, out_ref):
    half, rows = own_a_ref.shape[1:3]
    stripe = rows // Z
    for first, one, two in ((0, own_a_ref, w_up_ref), (half, own_b_ref, w_down_ref)):

        def add(pair, carry):
            totals = [one[0, b] + two[0, b].astype(jnp.float32) for b in (2 * pair, 2 * pair + 1)]
            at = pl.multiple_of((first + 2 * pair) * stripe, 2 * stripe)
            for z in range(Z):
                both = [total[z * stripe : (z + 1) * stripe] for total in totals]
                out_ref[z, pl.ds(at, 2 * stripe)] = jnp.concatenate(both, axis=0).astype(jnp.bfloat16)
            return carry

        lax.fori_loop(0, half // 2, add, 0, unroll=2)


def plane_sum(own_a, own_b, w_up, w_down):
    half, rows, columns = own_a.shape[1:]
    return pl.pallas_call(
        plane_kernel,
        out_shape=pltpu.VMEM((Z, 2 * half * rows // Z, columns), jnp.bfloat16),
        in_specs=[IN_VMEM] * 4,
        out_specs=IN_VMEM,
        compiler_params=PARAMS,
        name="plane_sum",
    )(own_a, own_b, w_up, w_down)


def select_kernel(devices, chosen_ref, *refs):
    out_ref = refs[-1]
    parts = []
    for ref in refs[:-1]:
        parts.append((jnp.sum(ref[...].astype(jnp.float32), axis=0) / devices).astype(jnp.bfloat16))
    out_ref[...] = dot16(chosen_ref[...], jnp.concatenate(parts, axis=0))


def select(chosen, pieces, devices):
    columns = pieces[0].shape[-1]
    return pl.pallas_call(
        lambda *refs: select_kernel(devices, *refs),
        out_shape=pltpu.VMEM((chosen.shape[0], columns), jnp.bfloat16),
        in_specs=[IN_VMEM] * (1 + len(pieces)),
        out_specs=IN_VMEM,
        compiler_params=PARAMS,
        name="select",
    )(chosen, *pieces)


def spread_kernel(in_ref, out_ref):
    stripe = in_ref.shape[1] // (Y * CORE * MOST)
    values = in_ref[...].astype(jnp.float32)
    for y in range(Y):
        for core in range(CORE):
            for slot in range(MOST):
                first = ((y * CORE + core) * MOST + slot) * stripe
                piece = values[:, first : first + stripe].reshape(Z * stripe, -1).astype(jnp.bfloat16)
                for m in range(slot, MP, MOST):
                    out_ref[y * MP + m, core] = piece


def spread(routed):
    stripe = routed.shape[1] // (Y * CORE * MOST)
    return pl.pallas_call(
        spread_kernel,
        out_shape=pltpu.VMEM((Y * MP, CORE, Z * stripe, routed.shape[2]), routed.dtype),
        in_specs=[IN_VMEM],
        out_specs=IN_VMEM,
        compiler_params=PARAMS,
        name="spread",
    )(routed)


def other_core_kernel(core_ref, in_ref, out_ref):
    for i in range(out_ref.shape[0]):
        out_ref[i] = in_ref[i, 1 - core_ref[0]]


def for_other_core(core, pieces):
    return pl.pallas_call(
        other_core_kernel,
        out_shape=pltpu.VMEM(pieces.shape[:1] + pieces.shape[2:], pieces.dtype),
        in_specs=[IN_SMEM, IN_VMEM],
        out_specs=IN_VMEM,
        compiler_params=PARAMS,
        name="for_other_core",
    )(core, pieces)


def place_kernel(band_ref, kept_ref, taken_ref, out_ref, sems):
    slot = band_ref[0] % MOST
    one = pltpu.make_async_copy(kept_ref, out_ref.at[slot], sems.at[0])
    two = pltpu.make_async_copy(taken_ref, out_ref.at[1 - slot], sems.at[1])
    one.start()
    two.start()
    one.wait()
    two.wait()


def place(band, kept, taken):
    return pl.pallas_call(
        place_kernel,
        out_shape=jax.ShapeDtypeStruct((MOST,) + kept.shape, kept.dtype),
        in_specs=[IN_SMEM, IN_VMEM, IN_VMEM],
        out_specs=IN_HBM,
        scratch_shapes=[pltpu.SemaphoreType.DMA((2,))],
        compiler_params=PARAMS,
        name="place",
    )(band, kept, taken)


def precondition_kernel(core_ref, band_ref, own_ref, other_ref, kept_ref, sent_ref, block_ref):
    own = band_ref[0]
    extent = block_ref.shape[0]
    rows, columns = other_ref.shape[1:]
    half = extent // CORE
    for y in range(Y):
        for j in range(MP):
            at = y * MP + (own ^ j)
            band = pl.ds(j * columns, columns)
            first = pl.multiple_of(core_ref[0] * half + y * rows, rows)
            block_ref[pl.ds(first, rows), band] = own_ref[at, core_ref[0]]
            first = pl.multiple_of((1 - core_ref[0]) * half + y * rows, rows)
            block_ref[pl.ds(first, rows), band] = other_ref[at]
    block = block_ref[...]
    row = lax.broadcasted_iota(jnp.int32, (extent, extent), 0)
    col = lax.broadcasted_iota(jnp.int32, (extent, extent), 1)
    five = jnp.where(row == col, jnp.float32(5.0), jnp.float32(0.0))
    left = lax.dot_general(block, block, (((1,), (1,)), ((), ())), preferred_element_type=jnp.float32)
    right = lax.dot_general(block, block, (((0,), (0,)), ((), ())), preferred_element_type=jnp.float32)
    moments, scales = [], []
    for stat in (left, right):
        total = jnp.sum(stat * stat, keepdims=True)
        scaling = 2.5 / jnp.sqrt(total + 1e-06)
        moments.append((scaling * stat).astype(jnp.bfloat16))
        scales.append(jnp.sqrt(jnp.sqrt(scaling)).astype(jnp.bfloat16).astype(jnp.float32))
    for iteration in range(ITERS):
        factors = [((five - m.astype(jnp.float32)) * 0.25).astype(jnp.bfloat16) for m in moments]
        if iteration == 0:
            roots = [(s * f.astype(jnp.float32)).astype(jnp.bfloat16) for s, f in zip(scales, factors)]
        elif iteration < ITERS - 1:
            roots = [dot16(r, f) for r, f in zip(roots, factors)]
        else:
            roots = [dot16(roots[0], factors[0]), dot16(roots[1], factors[1][:, : 2 * columns])]
        if iteration < ITERS - 1:
            squares = [dot16(f, f) for f in factors]
            fourths = [dot16(s, s) for s in squares]
            moments = [dot16(f, m) for f, m in zip(fourths, moments)]
    right_half = dot16(block, roots[1])
    product = (math.sqrt(extent) * dot(roots[0], right_half)).astype(jnp.bfloat16)
    kept_ref[...] = product[:, :columns]
    sent_ref[...] = product[:, columns:]


def on_device(grads, owner):
    local_grads = grads[0]
    block_count, extent, columns = local_grads.shape
    devices = Z * Y * CORE
    core = lax.axis_index("core").reshape(1).astype(jnp.int32)
    y = lax.axis_index("y").reshape(1).astype(jnp.int32)
    band = lax.axis_index("mp").reshape(1).astype(jnp.int32)
    chosen = selection(owner, devices, extent // devices)

    def swap(value):
        return lax.ppermute(value, "core", [(0, 1), (1, 0)])

    def up(value):
        return lax.ppermute(value, "y", [(i, (i + 1) % Y) for i in range(Y)])

    def down(value):
        return lax.ppermute(value, "y", [(i, (i - 1) % Y) for i in range(Y)])

    n = block_count // 2
    sent_far, kept_far = pieces_of(local_grads, core, y, (2,), "far")
    far = swap(sent_far)
    local_grads, kept_far = lax.optimization_barrier((local_grads, kept_far))
    sent_near, kept_near = pieces_of(local_grads, core, y, (1, 3), "near")
    near = swap(sent_near)
    local_grads, kept_near = lax.optimization_barrier((local_grads, kept_near))
    sent_own, kept_own = pieces_of(local_grads, core, y, (0,), "own")
    own = swap(sent_own)
    v2a, v2b = add_parts(
        [[(0, 0, 0, n), (1, 0, 0, n)], [(0, 0, n, n), (1, 0, n, n)]], (kept_far, far), jnp.bfloat16, "far_sum"
    )
    from_down, from_up = up(v2a), down(v2b)
    v1b, v3a = add_parts(
        [[(0, 0, n, n), (1, 0, n, n)], [(0, 1, 0, n), (1, 1, 0, n)]], (kept_near, near), jnp.bfloat16, "near_sum"
    )
    v_up, v_down = up(v1b), down(v3a)
    kept_near, near, v1b, v3a = lax.optimization_barrier((kept_near, near, v1b, v3a))
    w1a, w3b = add_parts(
        [[(0, 0, 0, n), (1, 0, 0, n), (2, 0, 0, n)], [(0, 1, n, n), (1, 1, n, n), (3, 0, 0, n)]],
        (kept_near, near, from_down, from_up),
        jnp.bfloat16,
        "relay_sum",
    )
    w_up, w_down = up(w1a), down(w3b)
    own_a, own_b = add_parts(
        [[(0, 0, 0, n), (1, 0, 0, n), (3, 0, 0, n)], [(0, 0, n, n), (1, 0, n, n), (2, 0, 0, n)]],
        (kept_own, own, v_up, v_down),
        jnp.float32,
        "own_sum",
    )
    own_a, own_b, chosen, band = lax.optimization_barrier((own_a, own_b, chosen, band))
    plane = plane_sum(own_a, own_b, w_up, w_down)
    pieces = [lax.all_to_all(plane, "z", split_axis=0, concat_axis=0, tiled=True)]
    outgoing = select(chosen, pieces, devices).reshape(Z, -1, columns)
    routed = lax.all_to_all(outgoing, "z", split_axis=0, concat_axis=0, tiled=True)
    spread_out = spread(routed)
    mine = lax.all_to_all(spread_out, ("y", "mp"), split_axis=0, concat_axis=0, tiled=True)
    other = swap(for_other_core(core, mine))

    result = pltpu.VMEM((extent, columns), jnp.bfloat16)
    kept, given = pl.pallas_call(
        precondition_kernel,
        out_shape=(result, result),
        in_specs=[IN_SMEM, IN_SMEM, IN_VMEM, IN_VMEM],
        out_specs=[IN_VMEM] * 2,
        scratch_shapes=[pltpu.VMEM((extent, extent), jnp.bfloat16)],
        compiler_params=LARGE,
        name="precondition",
    )(core, band, mine, other)
    taken = lax.ppermute(given, "mp", [(i, i ^ 1) for i in range(MP)])
    return place(band, kept, taken)


def solution(mesh):
    split = Mesh(mesh.devices.reshape(Z, Y, CORE, MP), ("z", "y", "core", "mp"))
    placed = (P(DP, None, None, "mp"), P())
    return jax.shard_map(
        on_device, mesh=split, in_specs=placed, out_specs=P(DP, None, "mp"), check_vma=False
    )
```

```python
import math

import jax
import jax.numpy as jnp
from jax import lax
from jax.experimental import pallas as pl
from jax.experimental.pallas import tpu as pltpu
from jax.sharding import Mesh, PartitionSpec as P

ITERS = 3
MOST = 2
Z, Y, CORE, MP = 8, 4, 2, 4
DP = ("z", "y", "core")
IN_VMEM = pl.BlockSpec(memory_space=pltpu.VMEM)
IN_SMEM = pl.BlockSpec(memory_space=pltpu.SMEM)
IN_HBM = pl.BlockSpec(memory_space=pltpu.HBM)
PARAMS = pltpu.CompilerParams(vmem_limit_bytes=12 * 1024 * 1024)
LARGE = pltpu.CompilerParams(vmem_limit_bytes=24 * 1024 * 1024)


def block_of_slots(owner, core):
    blocks = owner.shape[0]
    positions = jnp.arange(blocks, dtype=jnp.int32)
    earlier = (owner[None, :] == owner[:, None]) & (positions[None, :] < positions[:, None])
    slot_of = owner * MOST + jnp.sum(earlier.astype(jnp.int32), axis=1)
    local = jnp.arange(Z * Y * MOST, dtype=jnp.int32)
    wanted = (local // MOST * CORE + core) * MOST + local % MOST
    found = slot_of[None, :] == wanted[:, None]
    return jnp.sum(jnp.where(found, positions[None, :] + 1, 0), axis=1) - 1


def dot(a, b):
    return jnp.dot(a, b, preferred_element_type=jnp.float32)


def dot16(a, b):
    return dot(a, b).astype(jnp.bfloat16)


def pieces_of(grads, which_core, y, shifts, name):
    blocks, extent, columns = grads.shape
    half = extent // CORE
    rows = half // Y
    cuts = 4
    group = blocks // cuts

    def kernel(core_ref, y_ref, in_ref, *refs):
        outs, sems = refs[:-1], refs[-1]
        copies = []
        for out_ref, entry in zip(outs, shifts):
            for i, shift in enumerate(entry):
                first = pl.multiple_of(core_ref[0] * half + (y_ref[0] + shift) % Y * rows, rows)
                for cut in range(cuts):
                    some = pl.ds(cut * group, group)
                    source = in_ref.at[some, pl.ds(first, rows)]
                    copies.append(
                        pltpu.make_async_copy(source, out_ref.at[i, some], sems.at[len(copies)])
                    )
        for copy in copies:
            copy.start()
        for copy in copies:
            copy.wait()

    return pl.pallas_call(
        kernel,
        out_shape=[pltpu.VMEM((len(entry), blocks, rows, columns), grads.dtype) for entry in shifts],
        in_specs=[IN_SMEM, IN_SMEM, IN_HBM],
        out_specs=[IN_VMEM] * len(shifts),
        scratch_shapes=[pltpu.SemaphoreType.DMA((cuts * sum(len(entry) for entry in shifts),))],
        compiler_params=PARAMS,
        name=name,
    )(which_core, y, pltpu.with_memory_space_constraint(grads, pltpu.HBM))


def add_parts(parts, arrays, dtype, name):
    count = [entry[0][3] for entry in parts]
    rows, columns = arrays[0].shape[-2:]

    def kernel(*refs):
        ins, outs = refs[: len(arrays)], refs[len(arrays) :]
        for entry, out in zip(parts, outs):

            def add(b, carry):
                total = None
                for which, index, first, _ in entry:
                    value = ins[which][index, first + b].astype(jnp.float32)
                    total = value if total is None else total + value
                out[0, b] = total.astype(dtype)
                return carry

            lax.fori_loop(0, entry[0][3], add, 0, unroll=4)

    return pl.pallas_call(
        kernel,
        out_shape=[pltpu.VMEM((1, n, rows, columns), dtype) for n in count],
        in_specs=[IN_VMEM] * len(arrays),
        out_specs=[IN_VMEM] * len(parts),
        compiler_params=PARAMS,
        name=name,
    )(*arrays)


def plane_kernel(own_a_ref, own_b_ref, w_up_ref, w_down_ref, out_ref):
    half, rows = own_a_ref.shape[1:3]
    stripe = rows // Z
    for first, one, two in ((0, own_a_ref, w_up_ref), (half, own_b_ref, w_down_ref)):

        def add(pair, carry):
            totals = [one[0, b] + two[0, b].astype(jnp.float32) for b in (2 * pair, 2 * pair + 1)]
            at = pl.multiple_of((first + 2 * pair) * stripe, 2 * stripe)
            for z in range(Z):
                both = [total[z * stripe : (z + 1) * stripe] for total in totals]
                out_ref[z, pl.ds(at, 2 * stripe)] = jnp.concatenate(both, axis=0).astype(jnp.bfloat16)
            return carry

        lax.fori_loop(0, half // 2, add, 0, unroll=2)


def plane_sum(own_a, own_b, w_up, w_down):
    half, rows, columns = own_a.shape[1:]
    return pl.pallas_call(
        plane_kernel,
        out_shape=pltpu.VMEM((Z, 2 * half * rows // Z, columns), jnp.bfloat16),
        in_specs=[IN_VMEM] * 4,
        out_specs=IN_VMEM,
        compiler_params=PARAMS,
        name="plane_sum",
    )(own_a, own_b, w_up, w_down)


def mean_rows(pieces, devices):
    def kernel(in_ref, out_ref):
        out_ref[...] = (jnp.sum(in_ref[...].astype(jnp.float32), axis=0) / devices).astype(jnp.bfloat16)

    return pl.pallas_call(
        kernel,
        out_shape=pltpu.VMEM(pieces.shape[1:], pieces.dtype),
        in_specs=[IN_VMEM],
        out_specs=IN_VMEM,
        compiler_params=PARAMS,
        name="mean_rows",
    )(pieces)


def select_kernel(core_ref, block_ref, mine_ref, other_ref, out_ref, both_ref):
    blocks, rows, columns = both_ref.shape
    mine = mine_ref[...].astype(jnp.float32).reshape(blocks, rows // CORE, columns)
    other = other_ref[...].astype(jnp.float32).reshape(blocks, rows // CORE, columns)
    first = core_ref[0] == 0
    halves = [jnp.where(first, mine, other), jnp.where(first, other, mine)]
    both_ref[...] = jnp.concatenate(halves, axis=1).astype(jnp.bfloat16)
    for device in range(Z * Y):
        for slot in range(MOST):
            block = block_ref[device * MOST + slot]
            value = both_ref[jnp.maximum(block, 0)]
            out_ref[device, slot] = jnp.where(block >= 0, value, jnp.zeros_like(value))


def select(core, block_of, mine, other, blocks):
    rows = mine.shape[0] // blocks * CORE
    columns = mine.shape[1]
    return pl.pallas_call(
        select_kernel,
        out_shape=pltpu.VMEM((Z * Y, MOST, rows, columns), mine.dtype),
        in_specs=[IN_SMEM, IN_SMEM, IN_VMEM, IN_VMEM],
        out_specs=IN_VMEM,
        scratch_shapes=[pltpu.VMEM((blocks, rows, columns), mine.dtype)],
        compiler_params=PARAMS,
        name="select",
    )(core, block_of, mine, other)


def bands_kernel(band_ref, in_ref, own_ref, next_ref):
    slot = band_ref[0] % MOST
    devices, _, rows, _ = in_ref.shape
    for device in range(devices):
        part = pl.ds(device * rows, rows)
        own_ref[part] = in_ref[device, slot]
        next_ref[part] = in_ref[device, 1 - slot]


def bands_of(band, arrived):
    devices, _, rows, columns = arrived.shape
    shape = pltpu.VMEM((devices * rows, columns), arrived.dtype)
    return pl.pallas_call(
        bands_kernel,
        out_shape=(shape, shape),
        in_specs=[IN_SMEM, IN_VMEM],
        out_specs=[IN_VMEM] * 2,
        compiler_params=PARAMS,
        name="bands",
    )(band, arrived)


def precondition_kernel(band0_ref, band1_ref, band2_ref, band3_ref, kept_ref, sent_ref):
    extent, columns = kept_ref.shape
    block = jnp.concatenate([band0_ref[...], band1_ref[...], band2_ref[...], band3_ref[...]], axis=1)
    row = lax.broadcasted_iota(jnp.int32, (extent, extent), 0)
    col = lax.broadcasted_iota(jnp.int32, (extent, extent), 1)
    five = jnp.where(row == col, jnp.float32(5.0), jnp.float32(0.0))
    right = lax.dot_general(block, block, (((0,), (0,)), ((), ())), preferred_element_type=jnp.float32)
    left = lax.dot_general(block, block, (((1,), (1,)), ((), ())), preferred_element_type=jnp.float32)
    moments, scales = [], []
    for stat in (right, left):
        total = jnp.sum(stat * stat, keepdims=True)
        scaling = 2.5 / jnp.sqrt(total + 1e-06)
        moments.append((scaling * stat).astype(jnp.bfloat16))
        scales.append(jnp.sqrt(jnp.sqrt(scaling)).astype(jnp.bfloat16).astype(jnp.float32))
    factors = [((five - m.astype(jnp.float32)) * 0.25).astype(jnp.bfloat16) for m in moments]
    roots = [(s * f.astype(jnp.float32)).astype(jnp.bfloat16) for s, f in zip(scales, factors)]
    for iteration in range(ITERS - 1):
        squares = [dot16(f, f) for f in factors]
        if iteration > 0:
            roots = [dot16(r, f) for r, f in zip(roots, factors)]
        fourths = [dot16(s, s) for s in squares]
        moments = [dot16(f, m) for f, m in zip(fourths, moments)]
        factors = [((five - m.astype(jnp.float32)) * 0.25).astype(jnp.bfloat16) for m in moments]
    right_root = dot16(roots[0], factors[0][:, : 2 * columns])
    right_half = dot16(block, right_root)
    left_root = dot16(roots[1], factors[1])
    product = math.sqrt(extent) * dot(left_root, right_half)
    stripe = extent // (Z * Y * CORE)
    pieces = []
    for core in range(CORE):
        for y in range(Y):
            for z in range(Z):
                first = ((z * Y + y) * CORE + core) * stripe
                pieces.append(product[first : first + stripe])
    product = jnp.concatenate(pieces, axis=0).astype(jnp.bfloat16)
    kept_ref[...] = product[:, :columns]
    sent_ref[...] = product[:, columns:]


def place_kernel(band_ref, kept_ref, taken_ref, out_ref, sems):
    slot = band_ref[0] % MOST
    one = pltpu.make_async_copy(kept_ref, out_ref.at[slot], sems.at[0])
    two = pltpu.make_async_copy(taken_ref, out_ref.at[1 - slot], sems.at[1])
    one.start()
    two.start()
    one.wait()
    two.wait()


def place(band, kept, taken):
    return pl.pallas_call(
        place_kernel,
        out_shape=jax.ShapeDtypeStruct((MOST,) + kept.shape, kept.dtype),
        in_specs=[IN_SMEM, IN_VMEM, IN_VMEM],
        out_specs=IN_HBM,
        scratch_shapes=[pltpu.SemaphoreType.DMA((2,))],
        compiler_params=PARAMS,
        name="place",
    )(band, kept, taken)


def on_device(grads, owner):
    local_grads = grads[0]
    block_count, extent, columns = local_grads.shape
    devices = Z * Y * CORE
    core = lax.axis_index("core").reshape(1).astype(jnp.int32)
    y = lax.axis_index("y").reshape(1).astype(jnp.int32)
    band = lax.axis_index("mp").reshape(1).astype(jnp.int32)
    block_of = block_of_slots(owner, core)

    def swap(value):
        return lax.ppermute(value, "core", [(0, 1), (1, 0)])

    def up(value):
        return lax.ppermute(value, "y", [(i, (i + 1) % Y) for i in range(Y)])

    def down(value):
        return lax.ppermute(value, "y", [(i, (i - 1) % Y) for i in range(Y)])

    def along(value, shift):
        return lax.ppermute(value, "mp", [(i, (i + shift) % MP) for i in range(MP)])

    n = block_count // 2
    shifts = ((2,), (1, 3), (0,))
    far, near, own = (swap(sent) for sent in pieces_of(local_grads, 1 - core, y, shifts, "sent"))
    kept_far, kept_near, kept_own = pieces_of(local_grads, core, y, shifts, "kept")
    v2a, v2b = add_parts(
        [[(0, 0, 0, n), (1, 0, 0, n)], [(0, 0, n, n), (1, 0, n, n)]], (kept_far, far), jnp.bfloat16, "far_sum"
    )
    from_down, from_up = up(v2a), down(v2b)
    v1b, v3a = add_parts(
        [[(0, 0, n, n), (1, 0, n, n)], [(0, 1, 0, n), (1, 1, 0, n)]], (kept_near, near), jnp.bfloat16, "near_sum"
    )
    v_up, v_down = up(v1b), down(v3a)
    kept_near, near, v1b, v3a = lax.optimization_barrier((kept_near, near, v1b, v3a))
    (w1a,) = add_parts(
        [[(0, 0, 0, n), (1, 0, 0, n), (2, 0, 0, n)]], (kept_near, near, from_down), jnp.bfloat16, "relay_up"
    )
    (w3b,) = add_parts(
        [[(0, 1, n, n), (1, 1, n, n), (2, 0, 0, n)]], (kept_near, near, from_up), jnp.bfloat16, "relay_down"
    )
    w_up, w_down = up(w1a), down(w3b)
    own_a, own_b = add_parts(
        [[(0, 0, 0, n), (1, 0, 0, n), (3, 0, 0, n)], [(0, 0, n, n), (1, 0, n, n), (2, 0, 0, n)]],
        (kept_own, own, v_up, v_down),
        jnp.float32,
        "own_sum",
    )
    own_a, own_b, block_of, band = lax.optimization_barrier((own_a, own_b, block_of, band))
    plane = plane_sum(own_a, own_b, w_up, w_down)
    mine = mean_rows(lax.all_to_all(plane, "z", split_axis=0, concat_axis=0, tiled=True), devices)

    outgoing = select(core, block_of, mine, swap(mine), block_count)
    arrived = lax.all_to_all(outgoing, ("z", "y"), split_axis=0, concat_axis=0, tiled=True)
    own_band, next_band = bands_of(band, arrived)
    bands = [own_band, along(next_band, 3), along(own_band, 2), along(next_band, 1)]

    result = pltpu.VMEM((extent, columns), jnp.bfloat16)
    kept, given = pl.pallas_call(
        precondition_kernel,
        out_shape=(result, result),
        in_specs=[IN_VMEM] * MP,
        out_specs=[IN_VMEM] * 2,
        compiler_params=LARGE,
        name="precondition",
    )(*bands)
    return place(band, kept, along(given, 1))


def solution(mesh):
    split = Mesh(mesh.devices.reshape(Z, Y, CORE, MP), ("z", "y", "core", "mp"))
    placed = (P(DP, None, None, "mp"), P())
    return jax.shard_map(
        on_device, mesh=split, in_specs=placed, out_specs=P(DP, None, "mp"), check_vma=False
    )
```

```python
import math

import jax
import jax.numpy as jnp
from jax import lax
from jax.experimental import pallas as pl
from jax.experimental.pallas import tpu as pltpu
from jax.sharding import Mesh, PartitionSpec as P

ITERS = 3
MOST = 2
Z, Y, CORE, MP = 8, 4, 2, 4
DP = ("z", "y", "core")
IN_VMEM = pl.BlockSpec(memory_space=pltpu.VMEM)
IN_SMEM = pl.BlockSpec(memory_space=pltpu.SMEM)
IN_HBM = pl.BlockSpec(memory_space=pltpu.HBM)
PARAMS = pltpu.CompilerParams(vmem_limit_bytes=12 * 1024 * 1024)
LARGE = pltpu.CompilerParams(vmem_limit_bytes=24 * 1024 * 1024)


def selection(owner, core, blocks, stripe):
    positions = jnp.arange(blocks, dtype=jnp.int32)
    earlier = (owner[None, :] == owner[:, None]) & (positions[None, :] < positions[:, None])
    slot_of = owner * MOST + jnp.sum(earlier.astype(jnp.int32), axis=1)
    device = slot_of // MOST
    local = jnp.where(device % CORE == core, device // CORE * MOST + slot_of % MOST, Z * Y * MOST)
    half = jnp.arange(CORE, dtype=jnp.int32)[:, None, None]
    row = jnp.arange(stripe, dtype=jnp.int32)[None, None, :]
    wanted = ((local[None, :, None] * CORE + half) * stripe + row).reshape(1, CORE * blocks * stripe)
    rows = jnp.arange(Z * Y * MOST * CORE * stripe, dtype=jnp.int32)
    return (wanted == rows[:, None]).astype(jnp.bfloat16)


def dot(a, b):
    return jnp.dot(a, b, preferred_element_type=jnp.float32)


def dot16(a, b):
    return dot(a, b).astype(jnp.bfloat16)


def pieces_of(grads, which_core, y, shifts, name):
    blocks, extent, columns = grads.shape
    half = extent // CORE
    rows = half // Y
    cuts = 4
    group = blocks // cuts

    def kernel(core_ref, y_ref, in_ref, *refs):
        outs, sems = refs[:-1], refs[-1]
        copies = []
        for out_ref, entry in zip(outs, shifts):
            for i, shift in enumerate(entry):
                first = pl.multiple_of(core_ref[0] * half + (y_ref[0] + shift) % Y * rows, rows)
                for cut in range(cuts):
                    some = pl.ds(cut * group, group)
                    source = in_ref.at[some, pl.ds(first, rows)]
                    copies.append(
                        pltpu.make_async_copy(source, out_ref.at[i, some], sems.at[len(copies)])
                    )
        for copy in copies:
            copy.start()
        for copy in copies:
            copy.wait()

    return pl.pallas_call(
        kernel,
        out_shape=[pltpu.VMEM((len(entry), blocks, rows, columns), grads.dtype) for entry in shifts],
        in_specs=[IN_SMEM, IN_SMEM, IN_HBM],
        out_specs=[IN_VMEM] * len(shifts),
        scratch_shapes=[pltpu.SemaphoreType.DMA((cuts * sum(len(entry) for entry in shifts),))],
        compiler_params=PARAMS,
        name=name,
    )(which_core, y, pltpu.with_memory_space_constraint(grads, pltpu.HBM))


def add_parts(parts, arrays, dtype, name):
    count = [entry[0][3] for entry in parts]
    rows, columns = arrays[0].shape[-2:]

    def kernel(*refs):
        ins, outs = refs[: len(arrays)], refs[len(arrays) :]
        for entry, out in zip(parts, outs):

            def add(b, carry):
                total = None
                for which, index, first, _ in entry:
                    value = ins[which][index, first + b].astype(jnp.float32)
                    total = value if total is None else total + value
                out[0, b] = total.astype(dtype)
                return carry

            lax.fori_loop(0, entry[0][3], add, 0, unroll=4)

    return pl.pallas_call(
        kernel,
        out_shape=[pltpu.VMEM((1, n, rows, columns), dtype) for n in count],
        in_specs=[IN_VMEM] * len(arrays),
        out_specs=[IN_VMEM] * len(parts),
        compiler_params=PARAMS,
        name=name,
    )(*arrays)


def plane_kernel(z_ref, own_a_ref, own_b_ref, w_up_ref, w_down_ref, sent_a_ref, sent_b_ref, kept_ref):
    half, rows = own_a_ref.shape[1:3]
    stripe = rows // Z
    even = z_ref[0] % 2 == 0
    for first, one, two, sent in (
        (0, own_a_ref, w_up_ref, sent_a_ref),
        (half, own_b_ref, w_down_ref, sent_b_ref),
    ):

        def add(pair, carry):
            totals = [one[0, b] + two[0, b].astype(jnp.float32) for b in (2 * pair, 2 * pair + 1)]
            at = pl.multiple_of(2 * pair * stripe, 2 * stripe)
            for q in range(Z // 2):
                both = []
                for z in (2 * q, 2 * q + 1):
                    both.append(jnp.concatenate([t[z * stripe : (z + 1) * stripe] for t in totals], axis=0))
                sent[q, pl.ds(at, 2 * stripe)] = jnp.where(even, both[1], both[0]).astype(jnp.bfloat16)
                kept_ref[q, pl.ds(first * stripe + at, 2 * stripe)] = jnp.where(even, both[0], both[1])
            return carry

        lax.fori_loop(0, half // 2, add, 0, unroll=2)


def plane_sum(z, own_a, own_b, w_up, w_down):
    half, rows, columns = own_a.shape[1:]
    count = half * rows // Z
    sent = pltpu.VMEM((Z // 2, count, columns), jnp.bfloat16)
    return pl.pallas_call(
        plane_kernel,
        out_shape=(sent, sent, pltpu.VMEM((Z // 2, 2 * count, columns), jnp.float32)),
        in_specs=[IN_SMEM] + [IN_VMEM] * 4,
        out_specs=[IN_VMEM] * 3,
        compiler_params=PARAMS,
        name="plane_sum",
    )(z, own_a, own_b, w_up, w_down)


def parity_kernel(z_ref, kept_ref, a_ref, b_ref, far_ref, up_ref, down_ref, own_ref):
    count = a_ref.shape[1]
    for step, out_ref in ((2, far_ref), (1, up_ref), (3, down_ref), (0, own_ref)):
        q = (z_ref[0] // 2 + step) % (Z // 2)
        for first, ref in ((0, a_ref), (count, b_ref)):
            part = pl.ds(first, count)
            out_ref[part] = (kept_ref[q, part] + ref[q].astype(jnp.float32)).astype(out_ref.dtype)


def parity_sum(z, kept, a, b):
    shape = kept.shape[1:]
    sent = pltpu.VMEM(shape, jnp.bfloat16)
    return pl.pallas_call(
        parity_kernel,
        out_shape=(sent, sent, sent, pltpu.VMEM(shape, jnp.float32)),
        in_specs=[IN_SMEM] + [IN_VMEM] * 3,
        out_specs=[IN_VMEM] * 4,
        compiler_params=PARAMS,
        name="parity_sum",
    )(z, kept, a, b)


def mean_rows(own, received, devices):
    def kernel(own_ref, *refs):
        total = own_ref[...]
        for ref in refs[:-1]:
            total = total + ref[...].astype(jnp.float32)
        refs[-1][...] = (total / devices).astype(jnp.bfloat16)

    return pl.pallas_call(
        kernel,
        out_shape=pltpu.VMEM(own.shape, jnp.bfloat16),
        in_specs=[IN_VMEM] * (1 + len(received)),
        out_specs=IN_VMEM,
        compiler_params=PARAMS,
        name="mean_rows",
    )(own, *received)


def select_kernel(core_ref, chosen_ref, mine_ref, other_ref, out_ref):
    first = core_ref[0] == 0
    mine, other = mine_ref[...], other_ref[...]
    both = [jnp.where(first, mine, other), jnp.where(first, other, mine)]
    out_ref[...] = dot16(chosen_ref[...], jnp.concatenate(both, axis=0))


def select(core, chosen, mine, other):
    return pl.pallas_call(
        select_kernel,
        out_shape=pltpu.VMEM((chosen.shape[0], mine.shape[1]), mine.dtype),
        in_specs=[IN_SMEM, IN_VMEM, IN_VMEM, IN_VMEM],
        out_specs=IN_VMEM,
        compiler_params=PARAMS,
        name="select",
    )(core, chosen, mine, other)


def bands_kernel(band_ref, in_ref, own_ref, next_ref):
    slot = band_ref[0] % MOST
    devices, _, rows, _ = in_ref.shape
    for device in range(devices):
        part = pl.ds(device * rows, rows)
        own_ref[part] = in_ref[device, slot]
        next_ref[part] = in_ref[device, 1 - slot]


def bands_of(band, arrived):
    devices, _, rows, columns = arrived.shape
    shape = pltpu.VMEM((devices * rows, columns), arrived.dtype)
    return pl.pallas_call(
        bands_kernel,
        out_shape=(shape, shape),
        in_specs=[IN_SMEM, IN_VMEM],
        out_specs=[IN_VMEM] * 2,
        compiler_params=PARAMS,
        name="bands",
    )(band, arrived)


def precondition_kernel(band2_ref, band3_ref, band1_ref, band0_ref, kept_ref, sent_ref):
    extent, columns = kept_ref.shape
    block = jnp.concatenate([band0_ref[...], band1_ref[...], band2_ref[...], band3_ref[...]], axis=1)
    row = lax.broadcasted_iota(jnp.int32, (extent, extent), 0)
    col = lax.broadcasted_iota(jnp.int32, (extent, extent), 1)
    five = jnp.where(row == col, jnp.float32(5.0), jnp.float32(0.0))
    right = lax.dot_general(block, block, (((0,), (0,)), ((), ())), preferred_element_type=jnp.float32)
    left = lax.dot_general(block, block, (((1,), (1,)), ((), ())), preferred_element_type=jnp.float32)
    scaling = 2.5 / jnp.sqrt(jnp.sum(right * right, keepdims=True) + 1e-06)
    scale = jnp.sqrt(jnp.sqrt(scaling)).astype(jnp.bfloat16).astype(jnp.float32)
    moments = [(scaling * stat).astype(jnp.bfloat16) for stat in (right, left)]
    factors = [((five - m.astype(jnp.float32)) * 0.25).astype(jnp.bfloat16) for m in moments]
    roots = [(scale * f.astype(jnp.float32)).astype(jnp.bfloat16) for f in factors]
    for iteration in range(ITERS - 1):
        squares = [dot16(f, f) for f in factors]
        if iteration > 0:
            roots = [dot16(r, f) for r, f in zip(roots, factors)]
        fourths = [dot16(s, s) for s in squares]
        moments = [dot16(f, m) for f, m in zip(fourths, moments)]
        factors = [((five - m.astype(jnp.float32)) * 0.25).astype(jnp.bfloat16) for m in moments]
    right_root = dot16(roots[0], factors[0][:, : 2 * columns])
    right_half = dot16(block, right_root)
    left_root = dot16(roots[1], factors[1])
    product = math.sqrt(extent) * dot(left_root, right_half)
    stripe = extent // (Z * Y * CORE)
    pieces = []
    for core in range(CORE):
        for y in range(Y):
            for z in range(Z):
                first = ((z * Y + y) * CORE + core) * stripe
                pieces.append(product[first : first + stripe])
    product = jnp.concatenate(pieces, axis=0).astype(jnp.bfloat16)
    kept_ref[...] = product[:, :columns]
    sent_ref[...] = product[:, columns:]


def place_kernel(band_ref, kept_ref, taken_ref, out_ref, sems):
    slot = band_ref[0] % MOST
    cuts = sems.shape[1]
    rows = kept_ref.shape[0] // cuts
    copies = []
    for i, (source, to) in enumerate(((taken_ref, 1 - slot), (kept_ref, slot))):
        for cut in range(cuts):
            part = pl.ds(cut * rows, rows)
            copies.append(pltpu.make_async_copy(source.at[part], out_ref.at[to, part], sems.at[i, cut]))
    for copy in copies:
        copy.start()
    for copy in copies:
        copy.wait()


def place(band, kept, taken):
    return pl.pallas_call(
        place_kernel,
        out_shape=jax.ShapeDtypeStruct((MOST,) + kept.shape, kept.dtype),
        in_specs=[IN_SMEM, IN_VMEM, IN_VMEM],
        out_specs=IN_HBM,
        scratch_shapes=[pltpu.SemaphoreType.DMA((MOST, 4))],
        compiler_params=PARAMS,
        name="place",
    )(band, kept, taken)


def on_device(grads, owner):
    local_grads = grads[0]
    block_count, extent, columns = local_grads.shape
    devices = Z * Y * CORE
    core = lax.axis_index("core").reshape(1).astype(jnp.int32)
    y = lax.axis_index("y").reshape(1).astype(jnp.int32)
    z = lax.axis_index("z").reshape(1).astype(jnp.int32)
    band = lax.axis_index("mp").reshape(1).astype(jnp.int32)
    chosen = selection(owner, core, block_count, extent // devices)

    def swap(value):
        return lax.ppermute(value, "core", [(0, 1), (1, 0)])

    def up(value):
        return lax.ppermute(value, "y", [(i, (i + 1) % Y) for i in range(Y)])

    def down(value):
        return lax.ppermute(value, "y", [(i, (i - 1) % Y) for i in range(Y)])

    def along(value, shift):
        return lax.ppermute(value, "mp", [(i, (i + shift) % MP) for i in range(MP)])

    n = block_count // 2
    shifts = ((2,), (1, 3), (0,))
    far, near, own = (swap(sent) for sent in pieces_of(local_grads, 1 - core, y, shifts, "sent"))
    kept_far, kept_near, kept_own = pieces_of(local_grads, core, y, shifts, "kept")
    v2a, v2b = add_parts(
        [[(0, 0, 0, n), (1, 0, 0, n)], [(0, 0, n, n), (1, 0, n, n)]], (kept_far, far), jnp.bfloat16, "far_sum"
    )
    from_down, from_up = up(v2a), down(v2b)
    v1b, v3a = add_parts(
        [[(0, 0, n, n), (1, 0, n, n)], [(0, 1, 0, n), (1, 1, 0, n)]], (kept_near, near), jnp.bfloat16, "near_sum"
    )
    v_up, v_down = up(v1b), down(v3a)
    kept_near, near, v1b, v3a = lax.optimization_barrier((kept_near, near, v1b, v3a))
    (w1a,) = add_parts(
        [[(0, 0, 0, n), (1, 0, 0, n), (2, 0, 0, n)]], (kept_near, near, from_down), jnp.bfloat16, "relay_up"
    )
    w1a, kept_near = lax.optimization_barrier((w1a, kept_near))
    (w3b,) = add_parts(
        [[(0, 1, n, n), (1, 1, n, n), (2, 0, 0, n)]], (kept_near, near, from_up), jnp.bfloat16, "relay_down"
    )
    w_up, w_down = up(w1a), down(w3b)
    own_a, own_b = add_parts(
        [[(0, 0, 0, n), (1, 0, 0, n), (3, 0, 0, n)], [(0, 0, n, n), (1, 0, n, n), (2, 0, 0, n)]],
        (kept_own, own, v_up, v_down),
        jnp.float32,
        "own_sum",
    )
    own_a, own_b, chosen, band = lax.optimization_barrier((own_a, own_b, chosen, band))
    sent_a, sent_b, kept = plane_sum(z, own_a, own_b, w_up, w_down)
    got_a = lax.ppermute(sent_a, "z", [(i, i ^ 1) for i in range(Z)])
    got_b = lax.ppermute(sent_b, "z", [(i, (i - 1 + 2 * (i % 2)) % Z) for i in range(Z)])
    far, up_two, down_two, own = parity_sum(z, kept, got_a, got_b)
    received = [
        lax.ppermute(value, "z", [(i, (i + shift) % Z) for i in range(Z)])
        for value, shift in ((far, 4), (up_two, 2), (down_two, 6))
    ]
    mine = mean_rows(own, received, devices)

    outgoing = select(core, chosen, mine, swap(mine)).reshape(Z * Y, MOST, -1, columns)
    arrived = lax.all_to_all(outgoing, ("z", "y"), split_axis=0, concat_axis=0, tiled=True)
    own_band, next_band = bands_of(band, arrived)
    two, one, three = along(own_band, 2), along(next_band, 1), along(next_band, 3)

    result = pltpu.VMEM((extent, columns), jnp.bfloat16)
    kept, given = pl.pallas_call(
        precondition_kernel,
        out_shape=(result, result),
        in_specs=[IN_VMEM] * MP,
        out_specs=[IN_VMEM] * 2,
        compiler_params=LARGE,
        name="precondition",
    )(two, one, three, own_band)
    return place(band, kept, along(given, 1))


def solution(mesh):
    split = Mesh(mesh.devices.reshape(Z, Y, CORE, MP), ("z", "y", "core", "mp"))
    placed = (P(DP, None, None, "mp"), P())
    return jax.shard_map(
        on_device, mesh=split, in_specs=placed, out_specs=P(DP, None, "mp"), check_vma=False
    )
```

```python
import math

import jax
import jax.numpy as jnp
from jax import lax
from jax.experimental import pallas as pl
from jax.experimental.pallas import tpu as pltpu
from jax.sharding import Mesh, PartitionSpec as P

ITERS = 3
MOST = 2
Z, Y, CORE, MP = 8, 4, 2, 4
DP = ("z", "y", "core")
IN_VMEM = pl.BlockSpec(memory_space=pltpu.VMEM)
IN_SMEM = pl.BlockSpec(memory_space=pltpu.SMEM)
IN_HBM = pl.BlockSpec(memory_space=pltpu.HBM)
PARAMS = pltpu.CompilerParams(vmem_limit_bytes=12 * 1024 * 1024)
LARGE = pltpu.CompilerParams(vmem_limit_bytes=24 * 1024 * 1024)


def selection(owner, core, blocks, stripe):
    positions = jnp.arange(blocks, dtype=jnp.int32)
    earlier = (owner[None, :] == owner[:, None]) & (positions[None, :] < positions[:, None])
    slot_of = owner * MOST + jnp.sum(earlier.astype(jnp.int32), axis=1)
    device = slot_of // MOST
    local = jnp.where(device % CORE == core, device // CORE * MOST + slot_of % MOST, Z * Y * MOST)
    half = jnp.arange(CORE, dtype=jnp.int32)[:, None, None]
    row = jnp.arange(stripe, dtype=jnp.int32)[None, None, :]
    wanted = ((local[None, :, None] * CORE + half) * stripe + row).reshape(1, CORE * blocks * stripe)
    rows = jnp.arange(Z * Y * MOST * CORE * stripe, dtype=jnp.int32)
    return (wanted == rows[:, None]).astype(jnp.bfloat16)


def dot(a, b):
    return jnp.dot(a, b, preferred_element_type=jnp.float32)


def dot16(a, b):
    return dot(a, b).astype(jnp.bfloat16)


def piece_copies(core, y, in_ref, out_ref, sems, other, shift):
    blocks, rows = out_ref.shape[1:3]
    half = rows * Y
    which = 1 - core if other else core
    first = pl.multiple_of(which * half + (y + shift) % Y * rows, rows)
    cuts = sems.shape[0]
    group = blocks // cuts
    copies = []
    for cut in range(cuts):
        some = pl.ds(cut * group, group)
        source = in_ref.at[some, pl.ds(first, rows)]
        copies.append(pltpu.make_async_copy(source, out_ref.at[0, some], sems.at[cut]))
    return copies


def pieces_of(grads, core, y, entries, name):
    blocks, extent, columns = grads.shape
    rows = extent // CORE // Y

    def kernel(core_ref, y_ref, in_ref, *refs):
        outs, sems = refs[:-1], refs[-1]
        copies = []
        for i, (out_ref, (other, shift)) in enumerate(zip(outs, entries)):
            copies += piece_copies(core_ref[0], y_ref[0], in_ref, out_ref, sems.at[i], other, shift)
        for copy in copies:
            copy.start()
        for copy in copies:
            copy.wait()

    return pl.pallas_call(
        kernel,
        out_shape=[pltpu.VMEM((1, blocks, rows, columns), grads.dtype)] * len(entries),
        in_specs=[IN_SMEM, IN_SMEM, IN_HBM],
        out_specs=[IN_VMEM] * len(entries),
        scratch_shapes=[pltpu.SemaphoreType.DMA((len(entries), 4))],
        compiler_params=PARAMS,
        name=name,
    )(core, y, pltpu.with_memory_space_constraint(grads, pltpu.HBM))


def own_sum_kernel(core_ref, y_ref, grads_ref, got_ref, v_up_ref, v_down_ref, a_ref, b_ref, kept_ref, sems):
    copies = piece_copies(core_ref[0], y_ref[0], grads_ref, kept_ref, sems, False, 0)
    for copy in copies:
        copy.start()
    for copy in copies:
        copy.wait()
    half = a_ref.shape[1]
    for first, received, out in ((0, v_down_ref, a_ref), (half, v_up_ref, b_ref)):

        def add(b, carry):
            total = kept_ref[0, first + b].astype(jnp.float32) + got_ref[0, first + b].astype(jnp.float32)
            out[0, b] = total + received[0, b].astype(jnp.float32)
            return carry

        lax.fori_loop(0, half, add, 0, unroll=4)


def own_sum(grads, core, y, own, v_up, v_down):
    half, rows, columns = v_up.shape[1:]
    shape = pltpu.VMEM((1, half, rows, columns), jnp.float32)
    whole = pltpu.VMEM((1, 2 * half, rows, columns), grads.dtype)
    return pl.pallas_call(
        own_sum_kernel,
        out_shape=(shape, shape),
        in_specs=[IN_SMEM, IN_SMEM, IN_HBM, IN_VMEM, IN_VMEM, IN_VMEM],
        out_specs=[IN_VMEM] * 2,
        scratch_shapes=[whole, pltpu.SemaphoreType.DMA((4,))],
        compiler_params=PARAMS,
        name="own_sum",
    )(core, y, pltpu.with_memory_space_constraint(grads, pltpu.HBM), own, v_up, v_down)


def add_parts(parts, arrays, dtype, name):
    count = [entry[0][3] for entry in parts]
    rows, columns = arrays[0].shape[-2:]

    def kernel(*refs):
        ins, outs = refs[: len(arrays)], refs[len(arrays) :]
        for entry, out in zip(parts, outs):

            def add(b, carry):
                total = None
                for which, index, first, _ in entry:
                    value = ins[which][index, first + b].astype(jnp.float32)
                    total = value if total is None else total + value
                out[0, b] = total.astype(dtype)
                return carry

            lax.fori_loop(0, entry[0][3], add, 0, unroll=4)

    return pl.pallas_call(
        kernel,
        out_shape=[pltpu.VMEM((1, n, rows, columns), dtype) for n in count],
        in_specs=[IN_VMEM] * len(arrays),
        out_specs=[IN_VMEM] * len(parts),
        compiler_params=PARAMS,
        name=name,
    )(*arrays)


def plane_kernel(z_ref, own_a_ref, own_b_ref, w_up_ref, w_down_ref, sent_a_ref, sent_b_ref, kept_ref):
    half, rows = own_a_ref.shape[1:3]
    stripe = rows // Z
    even = z_ref[0] % 2 == 0
    for first, one, two, sent in (
        (0, own_a_ref, w_up_ref, sent_a_ref),
        (half, own_b_ref, w_down_ref, sent_b_ref),
    ):

        def add(pair, carry):
            totals = [one[0, b] + two[0, b].astype(jnp.float32) for b in (2 * pair, 2 * pair + 1)]
            at = pl.multiple_of(2 * pair * stripe, 2 * stripe)
            for q in range(Z // 2):
                both = []
                for z in (2 * q, 2 * q + 1):
                    both.append(jnp.concatenate([t[z * stripe : (z + 1) * stripe] for t in totals], axis=0))
                sent[q, pl.ds(at, 2 * stripe)] = jnp.where(even, both[1], both[0]).astype(jnp.bfloat16)
                kept_ref[q, pl.ds(first * stripe + at, 2 * stripe)] = jnp.where(even, both[0], both[1])
            return carry

        lax.fori_loop(0, half // 2, add, 0, unroll=2)


def plane_sum(z, own_a, own_b, w_up, w_down):
    half, rows, columns = own_a.shape[1:]
    count = half * rows // Z
    sent = pltpu.VMEM((Z // 2, count, columns), jnp.bfloat16)
    return pl.pallas_call(
        plane_kernel,
        out_shape=(sent, sent, pltpu.VMEM((Z // 2, 2 * count, columns), jnp.float32)),
        in_specs=[IN_SMEM] + [IN_VMEM] * 4,
        out_specs=[IN_VMEM] * 3,
        compiler_params=PARAMS,
        name="plane_sum",
    )(z, own_a, own_b, w_up, w_down)


def parity_kernel(z_ref, kept_ref, a_ref, b_ref, far_ref, outer_ref, inner_ref, own_ref):
    count = a_ref.shape[1]
    for change, out_ref in ((2, far_ref), (3, outer_ref), (1, inner_ref), (0, own_ref)):
        q = (z_ref[0] // 2) ^ change
        for first, ref in ((0, a_ref), (count, b_ref)):
            part = pl.ds(first, count)
            out_ref[part] = (kept_ref[q, part] + ref[q].astype(jnp.float32)).astype(out_ref.dtype)


def parity_sum(z, kept, a, b):
    shape = kept.shape[1:]
    sent = pltpu.VMEM(shape, jnp.bfloat16)
    return pl.pallas_call(
        parity_kernel,
        out_shape=(sent, sent, sent, pltpu.VMEM(shape, jnp.float32)),
        in_specs=[IN_SMEM] + [IN_VMEM] * 3,
        out_specs=[IN_VMEM] * 4,
        compiler_params=PARAMS,
        name="parity_sum",
    )(z, kept, a, b)


def mean_rows(own, received, devices):
    def kernel(own_ref, *refs):
        total = own_ref[...]
        for ref in refs[:-1]:
            total = total + ref[...].astype(jnp.float32)
        refs[-1][...] = (total / devices).astype(jnp.bfloat16)

    return pl.pallas_call(
        kernel,
        out_shape=pltpu.VMEM(own.shape, jnp.bfloat16),
        in_specs=[IN_VMEM] * (1 + len(received)),
        out_specs=IN_VMEM,
        compiler_params=PARAMS,
        name="mean_rows",
    )(own, *received)


def select_kernel(core_ref, chosen_ref, mine_ref, other_ref, out_ref):
    first = core_ref[0] == 0
    mine, other = mine_ref[...], other_ref[...]
    both = [jnp.where(first, mine, other), jnp.where(first, other, mine)]
    out_ref[...] = dot16(chosen_ref[...], jnp.concatenate(both, axis=0))


def select(core, chosen, mine, other):
    return pl.pallas_call(
        select_kernel,
        out_shape=pltpu.VMEM((chosen.shape[0], mine.shape[1]), mine.dtype),
        in_specs=[IN_SMEM, IN_VMEM, IN_VMEM, IN_VMEM],
        out_specs=IN_VMEM,
        compiler_params=PARAMS,
        name="select",
    )(core, chosen, mine, other)


def bands_kernel(band_ref, in_ref, own_ref, next_ref):
    slot = band_ref[0] % MOST
    devices, _, rows, _ = in_ref.shape
    for device in range(devices):
        part = pl.ds(device * rows, rows)
        own_ref[part] = in_ref[device, slot]
        next_ref[part] = in_ref[device, 1 - slot]


def bands_of(band, arrived):
    devices, _, rows, columns = arrived.shape
    shape = pltpu.VMEM((devices * rows, columns), arrived.dtype)
    return pl.pallas_call(
        bands_kernel,
        out_shape=(shape, shape),
        in_specs=[IN_SMEM, IN_VMEM],
        out_specs=[IN_VMEM] * 2,
        compiler_params=PARAMS,
        name="bands",
    )(band, arrived)


def precondition_kernel(same_ref, outer_ref, partner_ref, own_ref, kept_ref, sent_ref):
    extent, columns = kept_ref.shape
    block = jnp.concatenate([own_ref[...], partner_ref[...], same_ref[...], outer_ref[...]], axis=1)
    row = lax.broadcasted_iota(jnp.int32, (extent, extent), 0)
    col = lax.broadcasted_iota(jnp.int32, (extent, extent), 1)
    five = jnp.where(row == col, jnp.float32(5.0), jnp.float32(0.0))
    right = lax.dot_general(block, block, (((0,), (0,)), ((), ())), preferred_element_type=jnp.float32)
    left = lax.dot_general(block, block, (((1,), (1,)), ((), ())), preferred_element_type=jnp.float32)
    scaling = 2.5 / jnp.sqrt(jnp.sum(right * right, keepdims=True) + 1e-06)
    scale = jnp.sqrt(jnp.sqrt(scaling)).astype(jnp.bfloat16).astype(jnp.float32)
    moments = [(scaling * stat).astype(jnp.bfloat16) for stat in (right, left)]
    factors = [((five - m.astype(jnp.float32)) * 0.25).astype(jnp.bfloat16) for m in moments]
    roots = [(scale * f.astype(jnp.float32)).astype(jnp.bfloat16) for f in factors]
    for iteration in range(ITERS - 1):
        squares = [dot16(f, f) for f in factors]
        if iteration > 0:
            roots = [dot16(r, f) for r, f in zip(roots, factors)]
        fourths = [dot16(s, s) for s in squares]
        moments = [dot16(f, m) for f, m in zip(fourths, moments)]
        factors = [((five - m.astype(jnp.float32)) * 0.25).astype(jnp.bfloat16) for m in moments]
    right_root = dot16(roots[0], factors[0][:, : 2 * columns])
    right_half = dot16(block, right_root)
    left_root = dot16(roots[1], factors[1])
    product = math.sqrt(extent) * dot(left_root, right_half)
    stripe = extent // (Z * Y * CORE)
    pieces = []
    for core in range(CORE):
        for y in range(Y):
            for z in range(Z):
                first = ((z * Y + y) * CORE + core) * stripe
                pieces.append(product[first : first + stripe])
    product = jnp.concatenate(pieces, axis=0).astype(jnp.bfloat16)
    kept_ref[...] = product[:, :columns]
    sent_ref[...] = product[:, columns:]


def place_kernel(band_ref, kept_ref, taken_ref, out_ref, sems):
    slot = band_ref[0] % MOST
    cuts = sems.shape[1]
    rows = kept_ref.shape[0] // cuts
    copies = []
    for i, (source, to) in enumerate(((taken_ref, 1 - slot), (kept_ref, slot))):
        for cut in range(cuts):
            part = pl.ds(cut * rows, rows)
            copies.append(pltpu.make_async_copy(source.at[part], out_ref.at[to, part], sems.at[i, cut]))
    for copy in copies:
        copy.start()
    for copy in copies:
        copy.wait()


def place(band, kept, taken):
    return pl.pallas_call(
        place_kernel,
        out_shape=jax.ShapeDtypeStruct((MOST,) + kept.shape, kept.dtype),
        in_specs=[IN_SMEM, IN_VMEM, IN_VMEM],
        out_specs=IN_HBM,
        scratch_shapes=[pltpu.SemaphoreType.DMA((MOST, 4))],
        compiler_params=PARAMS,
        name="place",
    )(band, kept, taken)


def on_device(grads, owner):
    local_grads = grads[0]
    block_count, extent, columns = local_grads.shape
    devices = Z * Y * CORE
    core = lax.axis_index("core").reshape(1).astype(jnp.int32)
    y = lax.axis_index("y").reshape(1).astype(jnp.int32)
    z = lax.axis_index("z").reshape(1).astype(jnp.int32)
    band = lax.axis_index("mp").reshape(1).astype(jnp.int32)
    chosen = selection(owner, core, block_count, extent // devices)

    def swap(value):
        return lax.ppermute(value, "core", [(0, 1), (1, 0)])

    def up(value):
        return lax.ppermute(value, "y", [(i, (i + 1) % Y) for i in range(Y)])

    def down(value):
        return lax.ppermute(value, "y", [(i, (i - 1) % Y) for i in range(Y)])

    def along(value, to):
        return lax.ppermute(value, "mp", list(enumerate(to)))

    n = block_count // 2
    sent = pieces_of(local_grads, core, y, [(True, shift) for shift in (2, 1, 3)], "sent")
    far, near_up, near_down = (swap(piece) for piece in sent)
    kept_far, kept_up, kept_down = pieces_of(local_grads, core, y, [(False, shift) for shift in (2, 1, 3)], "kept")
    v2a, v2b = add_parts(
        [[(0, 0, 0, n), (1, 0, 0, n)], [(0, 0, n, n), (1, 0, n, n)]], (kept_far, far), jnp.bfloat16, "far_sum"
    )
    from_down, from_up = up(v2a), down(v2b)
    (v1b,) = add_parts([[(0, 0, n, n), (1, 0, n, n)]], (kept_up, near_up), jnp.bfloat16, "near_up")
    (v3a,) = add_parts([[(0, 0, 0, n), (1, 0, 0, n)]], (kept_down, near_down), jnp.bfloat16, "near_down")
    v_up, v_down = up(v1b), down(v3a)
    kept_up, kept_down, v1b, v3a, own_grads = lax.optimization_barrier(
        (kept_up, kept_down, v1b, v3a, local_grads)
    )
    (sent_own,) = pieces_of(own_grads, core, y, [(True, 0)], "own_piece")
    own = swap(sent_own)
    (w1a,) = add_parts(
        [[(0, 0, 0, n), (1, 0, 0, n), (2, 0, 0, n)]], (kept_up, near_up, from_down), jnp.bfloat16, "relay_up"
    )
    w1a, kept_down = lax.optimization_barrier((w1a, kept_down))
    (w3b,) = add_parts(
        [[(0, 0, n, n), (1, 0, n, n), (2, 0, 0, n)]], (kept_down, near_down, from_up), jnp.bfloat16, "relay_down"
    )
    w_up, w_down = up(w1a), down(w3b)
    own_a, own_b = own_sum(local_grads, core, y, own, v_up, v_down)
    own_a, own_b, chosen, band = lax.optimization_barrier((own_a, own_b, chosen, band))
    sent_a, sent_b, kept = plane_sum(z, own_a, own_b, w_up, w_down)
    got_a = lax.ppermute(sent_a, "z", [(i, i ^ 1) for i in range(Z)])
    got_b = lax.ppermute(sent_b, "z", [(i, (i - 1 + 2 * (i % 2)) % Z) for i in range(Z)])
    *sent, own = parity_sum(z, kept, got_a, got_b)
    received = [
        lax.ppermute(value, "z", [(i, i ^ change) for i in range(Z)]) for value, change in zip(sent, (4, 6, 2))
    ]
    mine = mean_rows(own, received, devices)

    outgoing = select(core, chosen, mine, swap(mine)).reshape(Z * Y, MOST, -1, columns)
    arrived = lax.all_to_all(outgoing, ("z", "y"), split_axis=0, concat_axis=0, tiled=True)
    own_band, next_band = bands_of(band, arrived)
    outer = along(next_band, (3, 2, 1, 0))
    same = along(own_band, (2, 3, 0, 1))
    partner = along(next_band, (1, 0, 3, 2))

    result = pltpu.VMEM((extent, columns), jnp.bfloat16)
    kept, given = pl.pallas_call(
        precondition_kernel,
        out_shape=(result, result),
        in_specs=[IN_VMEM] * MP,
        out_specs=[IN_VMEM] * 2,
        compiler_params=LARGE,
        name="precondition",
    )(same, outer, partner, own_band)
    return place(band, kept, along(given, (1, 0, 3, 2)))


def solution(mesh):
    split = Mesh(mesh.devices.reshape(Z, Y, CORE, MP), ("z", "y", "core", "mp"))
    placed = (P(DP, None, None, "mp"), P())
    return jax.shard_map(
        on_device, mesh=split, in_specs=placed, out_specs=P(DP, None, "mp"), check_vma=False
    )
```

```python
import math

import jax
import jax.numpy as jnp
from jax import lax
from jax.experimental import pallas as pl
from jax.experimental.pallas import tpu as pltpu
from jax.sharding import Mesh, PartitionSpec as P

ITERS = 3
MOST = 2
Z, Y, CORE, MP = 8, 4, 2, 4
DP = ("z", "y", "core")
IN_VMEM = pl.BlockSpec(memory_space=pltpu.VMEM)
IN_SMEM = pl.BlockSpec(memory_space=pltpu.SMEM)
IN_HBM = pl.BlockSpec(memory_space=pltpu.HBM)
PARAMS = pltpu.CompilerParams(vmem_limit_bytes=12 * 1024 * 1024)
LARGE = pltpu.CompilerParams(vmem_limit_bytes=24 * 1024 * 1024)


def selection(owner, core, blocks, stripe):
    positions = jnp.arange(blocks, dtype=jnp.int32)
    earlier = (owner[None, :] == owner[:, None]) & (positions[None, :] < positions[:, None])
    slot_of = owner * MOST + jnp.sum(earlier.astype(jnp.int32), axis=1)
    device = slot_of // MOST
    local = jnp.where(device % CORE == core, device // CORE * MOST + slot_of % MOST, Z * Y * MOST)
    half = jnp.arange(CORE, dtype=jnp.int32)[:, None, None]
    row = jnp.arange(stripe, dtype=jnp.int32)[None, None, :]
    wanted = ((local[None, :, None] * CORE + half) * stripe + row).reshape(1, CORE * blocks * stripe)
    rows = jnp.arange(Z * Y * MOST * CORE * stripe, dtype=jnp.int32)
    return (wanted == rows[:, None]).astype(jnp.bfloat16)


def dot(a, b):
    return jnp.dot(a, b, preferred_element_type=jnp.float32)


def dot16(a, b):
    return dot(a, b).astype(jnp.bfloat16)


def piece_copies(core, y, in_ref, out_ref, sems, other, shift):
    blocks, rows = out_ref.shape[1:3]
    half = rows * Y
    which = 1 - core if other else core
    first = pl.multiple_of(which * half + (y + shift) % Y * rows, rows)
    cuts = sems.shape[0]
    group = blocks // cuts
    copies = []
    for cut in range(cuts):
        some = pl.ds(cut * group, group)
        source = in_ref.at[some, pl.ds(first, rows)]
        copies.append(pltpu.make_async_copy(source, out_ref.at[0, some], sems.at[cut]))
    return copies


def pieces_of(grads, core, y, entries, name):
    blocks, extent, columns = grads.shape
    rows = extent // CORE // Y

    def kernel(core_ref, y_ref, in_ref, *refs):
        outs, sems = refs[:-1], refs[-1]
        copies = []
        for i, (out_ref, (other, shift)) in enumerate(zip(outs, entries)):
            copies += piece_copies(core_ref[0], y_ref[0], in_ref, out_ref, sems.at[i], other, shift)
        for copy in copies:
            copy.start()
        for copy in copies:
            copy.wait()

    return pl.pallas_call(
        kernel,
        out_shape=[pltpu.VMEM((1, blocks, rows, columns), grads.dtype)] * len(entries),
        in_specs=[IN_SMEM, IN_SMEM, IN_HBM],
        out_specs=[IN_VMEM] * len(entries),
        scratch_shapes=[pltpu.SemaphoreType.DMA((len(entries), 4))],
        compiler_params=PARAMS,
        name=name,
    )(core, y, pltpu.with_memory_space_constraint(grads, pltpu.HBM))


def own_sum_kernel(core_ref, y_ref, grads_ref, got_ref, v_up_ref, v_down_ref, a_ref, b_ref, kept_ref, sems):
    copies = piece_copies(core_ref[0], y_ref[0], grads_ref, kept_ref, sems, False, 0)
    for copy in copies:
        copy.start()
    for copy in copies:
        copy.wait()
    half = a_ref.shape[1]
    for first, received, out in ((0, v_down_ref, a_ref), (half, v_up_ref, b_ref)):

        def add(b, carry):
            total = kept_ref[0, first + b].astype(jnp.float32) + got_ref[0, first + b].astype(jnp.float32)
            out[0, b] = total + received[0, b].astype(jnp.float32)
            return carry

        lax.fori_loop(0, half, add, 0, unroll=4)


def own_sum(grads, core, y, own, v_up, v_down):
    half, rows, columns = v_up.shape[1:]
    shape = pltpu.VMEM((1, half, rows, columns), jnp.float32)
    whole = pltpu.VMEM((1, 2 * half, rows, columns), grads.dtype)
    return pl.pallas_call(
        own_sum_kernel,
        out_shape=(shape, shape),
        in_specs=[IN_SMEM, IN_SMEM, IN_HBM, IN_VMEM, IN_VMEM, IN_VMEM],
        out_specs=[IN_VMEM] * 2,
        scratch_shapes=[whole, pltpu.SemaphoreType.DMA((4,))],
        compiler_params=PARAMS,
        name="own_sum",
    )(core, y, pltpu.with_memory_space_constraint(grads, pltpu.HBM), own, v_up, v_down)


def add_parts(parts, arrays, dtype, name):
    count = [entry[0][3] for entry in parts]
    rows, columns = arrays[0].shape[-2:]

    def kernel(*refs):
        ins, outs = refs[: len(arrays)], refs[len(arrays) :]
        for entry, out in zip(parts, outs):

            def add(b, carry):
                total = None
                for which, index, first, _ in entry:
                    value = ins[which][index, first + b].astype(jnp.float32)
                    total = value if total is None else total + value
                out[0, b] = total.astype(dtype)
                return carry

            lax.fori_loop(0, entry[0][3], add, 0, unroll=4)

    return pl.pallas_call(
        kernel,
        out_shape=[pltpu.VMEM((1, n, rows, columns), dtype) for n in count],
        in_specs=[IN_VMEM] * len(arrays),
        out_specs=[IN_VMEM] * len(parts),
        compiler_params=PARAMS,
        name=name,
    )(*arrays)


def plane_kernel(z_ref, own_a_ref, own_b_ref, w_down_ref, w_up_ref, sent_a_ref, sent_b_ref, kept_ref):
    half, rows = own_a_ref.shape[1:3]
    stripe = rows // Z
    even = z_ref[0] % 2 == 0
    for first, one, two, sent in (
        (0, own_a_ref, w_up_ref, sent_a_ref),
        (half, own_b_ref, w_down_ref, sent_b_ref),
    ):

        def add(pair, carry):
            totals = [one[0, b] + two[0, b].astype(jnp.float32) for b in (2 * pair, 2 * pair + 1)]
            at = pl.multiple_of(2 * pair * stripe, 2 * stripe)
            for q in range(Z // 2):
                both = []
                for z in (2 * q, 2 * q + 1):
                    both.append(jnp.concatenate([t[z * stripe : (z + 1) * stripe] for t in totals], axis=0))
                sent[q, pl.ds(at, 2 * stripe)] = jnp.where(even, both[1], both[0]).astype(jnp.bfloat16)
                kept_ref[q, pl.ds(first * stripe + at, 2 * stripe)] = jnp.where(even, both[0], both[1])
            return carry

        lax.fori_loop(0, half // 2, add, 0, unroll=2)


def plane_sum(z, own_a, own_b, w_down, w_up):
    half, rows, columns = own_a.shape[1:]
    count = half * rows // Z
    sent = pltpu.VMEM((Z // 2, count, columns), jnp.bfloat16)
    return pl.pallas_call(
        plane_kernel,
        out_shape=(sent, sent, pltpu.VMEM((Z // 2, 2 * count, columns), jnp.float32)),
        in_specs=[IN_SMEM] + [IN_VMEM] * 4,
        out_specs=[IN_VMEM] * 3,
        compiler_params=PARAMS,
        name="plane_sum",
    )(z, own_a, own_b, w_down, w_up)


def parity_kernel(z_ref, kept_ref, a_ref, b_ref, far_ref, outer_ref, inner_ref, own_ref):
    count = a_ref.shape[1]
    for change, out_ref in ((2, far_ref), (3, outer_ref), (1, inner_ref), (0, own_ref)):
        q = (z_ref[0] // 2) ^ change
        for first, ref in ((0, a_ref), (count, b_ref)):
            part = pl.ds(first, count)
            out_ref[part] = (kept_ref[q, part] + ref[q].astype(jnp.float32)).astype(out_ref.dtype)


def parity_sum(z, kept, a, b):
    shape = kept.shape[1:]
    sent = pltpu.VMEM(shape, jnp.bfloat16)
    return pl.pallas_call(
        parity_kernel,
        out_shape=(sent, sent, sent, pltpu.VMEM(shape, jnp.float32)),
        in_specs=[IN_SMEM] + [IN_VMEM] * 3,
        out_specs=[IN_VMEM] * 4,
        compiler_params=PARAMS,
        name="parity_sum",
    )(z, kept, a, b)


def mean_rows(own, received, devices):
    def kernel(own_ref, *refs):
        total = own_ref[...]
        for ref in refs[:-1]:
            total = total + ref[...].astype(jnp.float32)
        refs[-1][...] = (total / devices).astype(jnp.bfloat16)

    return pl.pallas_call(
        kernel,
        out_shape=pltpu.VMEM(own.shape, jnp.bfloat16),
        in_specs=[IN_VMEM] * (1 + len(received)),
        out_specs=IN_VMEM,
        compiler_params=PARAMS,
        name="mean_rows",
    )(own, *received)


def select_kernel(core_ref, chosen_ref, mine_ref, other_ref, out_ref):
    first = core_ref[0] == 0
    mine, other = mine_ref[...], other_ref[...]
    both = [jnp.where(first, mine, other), jnp.where(first, other, mine)]
    out_ref[...] = dot16(chosen_ref[...], jnp.concatenate(both, axis=0))


def select(core, chosen, mine, other):
    return pl.pallas_call(
        select_kernel,
        out_shape=pltpu.VMEM((chosen.shape[0], mine.shape[1]), mine.dtype),
        in_specs=[IN_SMEM, IN_VMEM, IN_VMEM, IN_VMEM],
        out_specs=IN_VMEM,
        compiler_params=PARAMS,
        name="select",
    )(core, chosen, mine, other)


def bands_kernel(band_ref, in_ref, own_ref, next_ref):
    slot = band_ref[0] % MOST
    devices, _, rows, _ = in_ref.shape
    for device in range(devices):
        part = pl.ds(device * rows, rows)
        own_ref[part] = in_ref[device, slot]
        next_ref[part] = in_ref[device, 1 - slot]


def bands_of(band, arrived):
    devices, _, rows, columns = arrived.shape
    shape = pltpu.VMEM((devices * rows, columns), arrived.dtype)
    return pl.pallas_call(
        bands_kernel,
        out_shape=(shape, shape),
        in_specs=[IN_SMEM, IN_VMEM],
        out_specs=[IN_VMEM] * 2,
        compiler_params=PARAMS,
        name="bands",
    )(band, arrived)


def precondition_kernel(same_ref, outer_ref, partner_ref, own_ref, kept_ref, sent_ref):
    extent, columns = kept_ref.shape
    block = jnp.concatenate([own_ref[...], partner_ref[...], same_ref[...], outer_ref[...]], axis=1)
    row = lax.broadcasted_iota(jnp.int32, (extent, extent), 0)
    col = lax.broadcasted_iota(jnp.int32, (extent, extent), 1)
    five = jnp.where(row == col, jnp.float32(5.0), jnp.float32(0.0))
    right = lax.dot_general(block, block, (((0,), (0,)), ((), ())), preferred_element_type=jnp.float32)
    left = lax.dot_general(block, block, (((1,), (1,)), ((), ())), preferred_element_type=jnp.float32)
    scaling = 2.5 / jnp.sqrt(jnp.sum(right * right, keepdims=True) + 1e-06)
    scale = jnp.sqrt(jnp.sqrt(scaling)).astype(jnp.bfloat16).astype(jnp.float32)
    moments = [(scaling * stat).astype(jnp.bfloat16) for stat in (right, left)]
    factors = [((five - m.astype(jnp.float32)) * 0.25).astype(jnp.bfloat16) for m in moments]
    roots = [(scale * f.astype(jnp.float32)).astype(jnp.bfloat16) for f in factors]
    for iteration in range(ITERS - 1):
        squares = [dot16(f, f) for f in factors]
        if iteration > 0:
            roots = [dot16(r, f) for r, f in zip(roots, factors)]
        fourths = [dot16(s, s) for s in squares]
        moments = [dot16(f, m) for f, m in zip(fourths, moments)]
        factors = [((five - m.astype(jnp.float32)) * 0.25).astype(jnp.bfloat16) for m in moments]
    right_root = dot16(roots[0], factors[0][:, : 2 * columns])
    right_half = dot16(block, right_root)
    left_root = dot16(roots[1], factors[1])
    product = math.sqrt(extent) * dot(left_root, right_half)
    stripe = extent // (Z * Y * CORE)
    pieces = []
    for core in range(CORE):
        for y in range(Y):
            for z in range(Z):
                first = ((z * Y + y) * CORE + core) * stripe
                pieces.append(product[first : first + stripe])
    product = jnp.concatenate(pieces, axis=0).astype(jnp.bfloat16)
    kept_ref[...] = product[:, :columns]
    sent_ref[...] = product[:, columns:]


def place_kernel(band_ref, kept_ref, taken_ref, out_ref, sems):
    slot = band_ref[0] % MOST
    cuts = sems.shape[1]
    rows = kept_ref.shape[0] // cuts
    copies = []
    for i, (source, to) in enumerate(((taken_ref, 1 - slot), (kept_ref, slot))):
        for cut in range(cuts):
            part = pl.ds(cut * rows, rows)
            copies.append(pltpu.make_async_copy(source.at[part], out_ref.at[to, part], sems.at[i, cut]))
    for copy in copies:
        copy.start()
    for copy in copies:
        copy.wait()


def place(band, kept, taken):
    return pl.pallas_call(
        place_kernel,
        out_shape=jax.ShapeDtypeStruct((MOST,) + kept.shape, kept.dtype),
        in_specs=[IN_SMEM, IN_VMEM, IN_VMEM],
        out_specs=IN_HBM,
        scratch_shapes=[pltpu.SemaphoreType.DMA((MOST, 4))],
        compiler_params=PARAMS,
        name="place",
    )(band, kept, taken)


def on_device(grads, owner):
    local_grads = grads[0]
    block_count, extent, columns = local_grads.shape
    devices = Z * Y * CORE
    core = lax.axis_index("core").reshape(1).astype(jnp.int32)
    y = lax.axis_index("y").reshape(1).astype(jnp.int32)
    z = lax.axis_index("z").reshape(1).astype(jnp.int32)
    band = lax.axis_index("mp").reshape(1).astype(jnp.int32)
    chosen = selection(owner, core, block_count, extent // devices)

    def swap(value):
        return lax.ppermute(value, "core", [(0, 1), (1, 0)])

    def up(value):
        return lax.ppermute(value, "y", [(i, (i + 1) % Y) for i in range(Y)])

    def down(value):
        return lax.ppermute(value, "y", [(i, (i - 1) % Y) for i in range(Y)])

    def along(value, to):
        return lax.ppermute(value, "mp", list(enumerate(to)))

    n = block_count // 2
    sent = pieces_of(local_grads, core, y, [(True, shift) for shift in (2, 1, 3)], "sent")
    far, near_up, near_down = (swap(piece) for piece in sent)
    kept_far, kept_up, kept_down, sent_own = pieces_of(
        local_grads, core, y, [(False, shift) for shift in (2, 1, 3)] + [(True, 0)], "kept"
    )
    own = swap(sent_own)
    v2a, v2b = add_parts(
        [[(0, 0, 0, n), (1, 0, 0, n)], [(0, 0, n, n), (1, 0, n, n)]], (kept_far, far), jnp.bfloat16, "far_sum"
    )
    from_down, from_up = up(v2a), down(v2b)
    (v1b,) = add_parts([[(0, 0, n, n), (1, 0, n, n)]], (kept_up, near_up), jnp.bfloat16, "near_up")
    (v3a,) = add_parts([[(0, 0, 0, n), (1, 0, 0, n)]], (kept_down, near_down), jnp.bfloat16, "near_down")
    v_up, v_down = up(v1b), down(v3a)
    kept_up, kept_down, v1b, v3a = lax.optimization_barrier((kept_up, kept_down, v1b, v3a))
    (w1a,) = add_parts(
        [[(0, 0, 0, n), (1, 0, 0, n), (2, 0, 0, n)]], (kept_up, near_up, from_down), jnp.bfloat16, "relay_up"
    )
    (w3b,) = add_parts(
        [[(0, 0, n, n), (1, 0, n, n), (2, 0, 0, n)]], (kept_down, near_down, from_up), jnp.bfloat16, "relay_down"
    )
    w_up, w_down = up(w1a), down(w3b)
    own_a, own_b = own_sum(local_grads, core, y, own, v_up, v_down)
    own_a, own_b, chosen, band = lax.optimization_barrier((own_a, own_b, chosen, band))
    sent_a, sent_b, kept = plane_sum(z, own_a, own_b, w_down, w_up)
    got_a = lax.ppermute(sent_a, "z", [(i, i ^ 1) for i in range(Z)])
    got_b = lax.ppermute(sent_b, "z", [(i, (i - 1 + 2 * (i % 2)) % Z) for i in range(Z)])
    *sent, own = parity_sum(z, kept, got_a, got_b)
    received = [
        lax.ppermute(value, "z", [(i, i ^ change) for i in range(Z)]) for value, change in zip(sent, (4, 6, 2))
    ]
    mine = mean_rows(own, received, devices)

    outgoing = select(core, chosen, mine, swap(mine)).reshape(Z * Y, MOST, -1, columns)
    arrived = lax.all_to_all(outgoing, ("z", "y"), split_axis=0, concat_axis=0, tiled=True)
    own_band, next_band = bands_of(band, arrived)
    outer = along(next_band, (3, 2, 1, 0))
    same = along(own_band, (2, 3, 0, 1))
    partner = along(next_band, (1, 0, 3, 2))

    result = pltpu.VMEM((extent, columns), jnp.bfloat16)
    kept, given = pl.pallas_call(
        precondition_kernel,
        out_shape=(result, result),
        in_specs=[IN_VMEM] * MP,
        out_specs=[IN_VMEM] * 2,
        compiler_params=LARGE,
        name="precondition",
    )(same, outer, partner, own_band)
    return place(band, kept, along(given, (1, 0, 3, 2)))


def solution(mesh):
    split = Mesh(mesh.devices.reshape(Z, Y, CORE, MP), ("z", "y", "core", "mp"))
    placed = (P(DP, None, None, "mp"), P())
    return jax.shard_map(
        on_device, mesh=split, in_specs=placed, out_specs=P(DP, None, "mp"), check_vma=False
    )
```

```python
import math

import jax
import jax.numpy as jnp
from jax import lax
from jax.experimental import pallas as pl
from jax.experimental.pallas import tpu as pltpu
from jax.sharding import Mesh, PartitionSpec as P

ITERS = 3
MOST = 2
Z, Y, CORE, MP = 8, 4, 2, 4
DP = ("z", "y", "core")
IN_VMEM = pl.BlockSpec(memory_space=pltpu.VMEM)
IN_SMEM = pl.BlockSpec(memory_space=pltpu.SMEM)
IN_HBM = pl.BlockSpec(memory_space=pltpu.HBM)
PARAMS = pltpu.CompilerParams(vmem_limit_bytes=12 * 1024 * 1024)
LARGE = pltpu.CompilerParams(vmem_limit_bytes=24 * 1024 * 1024)


def selection(owner, core, blocks, stripe):
    positions = jnp.arange(blocks, dtype=jnp.int32)
    earlier = (owner[None, :] == owner[:, None]) & (positions[None, :] < positions[:, None])
    slot_of = owner * MOST + jnp.sum(earlier.astype(jnp.int32), axis=1)
    device = slot_of // MOST
    local = jnp.where(device % CORE == core, device // CORE * MOST + slot_of % MOST, Z * Y * MOST)
    half = jnp.arange(CORE, dtype=jnp.int32)[:, None, None]
    row = jnp.arange(stripe, dtype=jnp.int32)[None, None, :]
    wanted = ((local[None, :, None] * CORE + half) * stripe + row).reshape(1, CORE * blocks * stripe)
    rows = jnp.arange(Z * Y * MOST * CORE * stripe, dtype=jnp.int32)
    return (wanted == rows[:, None]).astype(jnp.bfloat16)


def dot(a, b):
    return jnp.dot(a, b, preferred_element_type=jnp.float32)


def dot16(a, b):
    return dot(a, b).astype(jnp.bfloat16)


def piece_copies(core, y, in_ref, out_ref, sems, other, shift):
    blocks, rows = out_ref.shape[1:3]
    half = rows * Y
    which = 1 - core if other else core
    first = pl.multiple_of(which * half + (y + shift) % Y * rows, rows)
    cuts = sems.shape[0]
    group = blocks // cuts
    copies = []
    for cut in range(cuts):
        some = pl.ds(cut * group, group)
        source = in_ref.at[some, pl.ds(first, rows)]
        copies.append(pltpu.make_async_copy(source, out_ref.at[0, some], sems.at[cut]))
    return copies


def pieces_of(grads, core, y, entries, name):
    blocks, extent, columns = grads.shape
    rows = extent // CORE // Y

    def kernel(core_ref, y_ref, in_ref, *refs):
        outs, sems = refs[:-1], refs[-1]
        copies = []
        for i, (out_ref, (other, shift)) in enumerate(zip(outs, entries)):
            copies += piece_copies(core_ref[0], y_ref[0], in_ref, out_ref, sems.at[i], other, shift)
        for copy in copies:
            copy.start()
        for copy in copies:
            copy.wait()

    return pl.pallas_call(
        kernel,
        out_shape=[pltpu.VMEM((1, blocks, rows, columns), grads.dtype)] * len(entries),
        in_specs=[IN_SMEM, IN_SMEM, IN_HBM],
        out_specs=[IN_VMEM] * len(entries),
        scratch_shapes=[pltpu.SemaphoreType.DMA((len(entries), 4))],
        compiler_params=PARAMS,
        name=name,
    )(core, y, pltpu.with_memory_space_constraint(grads, pltpu.HBM))


def own_sum_kernel(core_ref, y_ref, grads_ref, got_ref, v_up_ref, v_down_ref, a_ref, b_ref, kept_ref, sems):
    copies = piece_copies(core_ref[0], y_ref[0], grads_ref, kept_ref, sems, False, 0)
    for copy in copies:
        copy.start()
    for copy in copies:
        copy.wait()
    half = a_ref.shape[1]
    for first, received, out in ((0, v_down_ref, a_ref), (half, v_up_ref, b_ref)):

        def add(b, carry):
            total = kept_ref[0, first + b].astype(jnp.float32) + got_ref[0, first + b].astype(jnp.float32)
            out[0, b] = total + received[0, b].astype(jnp.float32)
            return carry

        lax.fori_loop(0, half, add, 0, unroll=4)


def own_sum(grads, core, y, own, v_up, v_down):
    half, rows, columns = v_up.shape[1:]
    shape = pltpu.VMEM((1, half, rows, columns), jnp.float32)
    whole = pltpu.VMEM((1, 2 * half, rows, columns), grads.dtype)
    return pl.pallas_call(
        own_sum_kernel,
        out_shape=(shape, shape),
        in_specs=[IN_SMEM, IN_SMEM, IN_HBM, IN_VMEM, IN_VMEM, IN_VMEM],
        out_specs=[IN_VMEM] * 2,
        scratch_shapes=[whole, pltpu.SemaphoreType.DMA((4,))],
        compiler_params=PARAMS,
        name="own_sum",
    )(core, y, pltpu.with_memory_space_constraint(grads, pltpu.HBM), own, v_up, v_down)


def add_parts(parts, arrays, dtype, name):
    count = [entry[0][3] for entry in parts]
    rows, columns = arrays[0].shape[-2:]

    def kernel(*refs):
        ins, outs = refs[: len(arrays)], refs[len(arrays) :]
        for entry, out in zip(parts, outs):

            def add(b, carry):
                total = None
                for which, index, first, _ in entry:
                    value = ins[which][index, first + b].astype(jnp.float32)
                    total = value if total is None else total + value
                out[0, b] = total.astype(dtype)
                return carry

            lax.fori_loop(0, entry[0][3], add, 0, unroll=4)

    return pl.pallas_call(
        kernel,
        out_shape=[pltpu.VMEM((1, n, rows, columns), dtype) for n in count],
        in_specs=[IN_VMEM] * len(arrays),
        out_specs=[IN_VMEM] * len(parts),
        compiler_params=PARAMS,
        name=name,
    )(*arrays)


def plane_kernel(z_ref, own_a_ref, own_b_ref, w_down_ref, w_up_ref, sent_a_ref, sent_b_ref, kept_ref):
    half, rows = own_a_ref.shape[1:3]
    stripe = rows // Z
    even = z_ref[0] % 2 == 0
    for first, one, two, sent in (
        (0, own_a_ref, w_up_ref, sent_a_ref),
        (half, own_b_ref, w_down_ref, sent_b_ref),
    ):

        def add(pair, carry):
            totals = [one[0, b] + two[0, b].astype(jnp.float32) for b in (2 * pair, 2 * pair + 1)]
            at = pl.multiple_of(2 * pair * stripe, 2 * stripe)
            for q in range(Z // 2):
                both = []
                for z in (2 * q, 2 * q + 1):
                    both.append(jnp.concatenate([t[z * stripe : (z + 1) * stripe] for t in totals], axis=0))
                sent[q, pl.ds(at, 2 * stripe)] = jnp.where(even, both[1], both[0]).astype(jnp.bfloat16)
                kept_ref[q, pl.ds(first * stripe + at, 2 * stripe)] = jnp.where(even, both[0], both[1])
            return carry

        lax.fori_loop(0, half // 2, add, 0, unroll=2)


def plane_sum(z, own_a, own_b, w_down, w_up):
    half, rows, columns = own_a.shape[1:]
    count = half * rows // Z
    sent = pltpu.VMEM((Z // 2, count, columns), jnp.bfloat16)
    return pl.pallas_call(
        plane_kernel,
        out_shape=(sent, sent, pltpu.VMEM((Z // 2, 2 * count, columns), jnp.float32)),
        in_specs=[IN_SMEM] + [IN_VMEM] * 4,
        out_specs=[IN_VMEM] * 3,
        compiler_params=PARAMS,
        name="plane_sum",
    )(z, own_a, own_b, w_down, w_up)


def parity_kernel(z_ref, kept_ref, a_ref, b_ref, far_ref, outer_ref, inner_ref, own_ref):
    count = a_ref.shape[1]
    for change, out_ref in ((2, far_ref), (3, outer_ref), (1, inner_ref), (0, own_ref)):
        q = (z_ref[0] // 2) ^ change
        for first, ref in ((0, a_ref), (count, b_ref)):
            part = pl.ds(first, count)
            out_ref[part] = (kept_ref[q, part] + ref[q].astype(jnp.float32)).astype(out_ref.dtype)


def parity_sum(z, kept, a, b):
    shape = kept.shape[1:]
    sent = pltpu.VMEM(shape, jnp.bfloat16)
    return pl.pallas_call(
        parity_kernel,
        out_shape=(sent, sent, sent, pltpu.VMEM(shape, jnp.float32)),
        in_specs=[IN_SMEM] + [IN_VMEM] * 3,
        out_specs=[IN_VMEM] * 4,
        compiler_params=PARAMS,
        name="parity_sum",
    )(z, kept, a, b)


def mean_rows(own, received, devices):
    def kernel(own_ref, *refs):
        total = own_ref[...]
        for ref in refs[:-1]:
            total = total + ref[...].astype(jnp.float32)
        refs[-1][...] = (total / devices).astype(jnp.bfloat16)

    return pl.pallas_call(
        kernel,
        out_shape=pltpu.VMEM(own.shape, jnp.bfloat16),
        in_specs=[IN_VMEM] * (1 + len(received)),
        out_specs=IN_VMEM,
        compiler_params=PARAMS,
        name="mean_rows",
    )(own, *received)


def select_kernel(core_ref, chosen_ref, mine_ref, other_ref, out_ref):
    first = core_ref[0] == 0
    mine, other = mine_ref[...], other_ref[...]
    both = [jnp.where(first, mine, other), jnp.where(first, other, mine)]
    out_ref[...] = dot16(chosen_ref[...], jnp.concatenate(both, axis=0))


def select(core, chosen, mine, other):
    return pl.pallas_call(
        select_kernel,
        out_shape=pltpu.VMEM((chosen.shape[0], mine.shape[1]), mine.dtype),
        in_specs=[IN_SMEM, IN_VMEM, IN_VMEM, IN_VMEM],
        out_specs=IN_VMEM,
        compiler_params=PARAMS,
        name="select",
    )(core, chosen, mine, other)


def bands_kernel(band_ref, in_ref, own_ref, next_ref):
    slot = band_ref[0] % MOST
    devices, _, rows, _ = in_ref.shape
    for device in range(devices):
        part = pl.ds(device * rows, rows)
        own_ref[part] = in_ref[device, slot]
        next_ref[part] = in_ref[device, 1 - slot]


def bands_of(band, arrived):
    devices, _, rows, columns = arrived.shape
    shape = pltpu.VMEM((devices * rows, columns), arrived.dtype)
    return pl.pallas_call(
        bands_kernel,
        out_shape=(shape, shape),
        in_specs=[IN_SMEM, IN_VMEM],
        out_specs=[IN_VMEM] * 2,
        compiler_params=PARAMS,
        name="bands",
    )(band, arrived)


def precondition_kernel(same_ref, outer_ref, partner_ref, own_ref, kept_ref, sent_ref):
    extent, columns = kept_ref.shape
    block = jnp.concatenate([own_ref[...], partner_ref[...], same_ref[...], outer_ref[...]], axis=1)
    row = lax.broadcasted_iota(jnp.int32, (extent, extent), 0)
    col = lax.broadcasted_iota(jnp.int32, (extent, extent), 1)
    five = jnp.where(row == col, jnp.float32(5.0), jnp.float32(0.0))
    right = lax.dot_general(block, block, (((0,), (0,)), ((), ())), preferred_element_type=jnp.float32)
    left = lax.dot_general(block, block, (((1,), (1,)), ((), ())), preferred_element_type=jnp.float32)
    scaling = 2.5 / jnp.sqrt(jnp.sum(right * right, keepdims=True) + 1e-06)
    scale = jnp.sqrt(jnp.sqrt(scaling)).astype(jnp.bfloat16).astype(jnp.float32)
    moments = [(scaling * stat).astype(jnp.bfloat16) for stat in (right, left)]
    factors = [((five - m.astype(jnp.float32)) * 0.25).astype(jnp.bfloat16) for m in moments]
    roots = [(scale * f.astype(jnp.float32)).astype(jnp.bfloat16) for f in factors]
    for iteration in range(ITERS - 1):
        squares = [dot16(f, f) for f in factors]
        if iteration > 0:
            roots = [dot16(r, f) for r, f in zip(roots, factors)]
        fourths = [dot16(s, s) for s in squares]
        moments = [dot16(f, m) for f, m in zip(fourths, moments)]
        factors = [((five - m.astype(jnp.float32)) * 0.25).astype(jnp.bfloat16) for m in moments]
    right_root = dot16(roots[0], factors[0][:, : 2 * columns])
    right_half = dot16(block, right_root)
    left_root = dot16(roots[1], factors[1])
    product = math.sqrt(extent) * dot(left_root, right_half)
    stripe = extent // (Z * Y * CORE)
    pieces = []
    for core in range(CORE):
        for y in range(Y):
            for z in range(Z):
                first = ((z * Y + y) * CORE + core) * stripe
                pieces.append(product[first : first + stripe])
    product = jnp.concatenate(pieces, axis=0).astype(jnp.bfloat16)
    kept_ref[...] = product[:, :columns]
    sent_ref[...] = product[:, columns:]


def place_kernel(band_ref, kept_ref, taken_ref, out_ref, sems):
    slot = band_ref[0] % MOST
    cuts = sems.shape[1]
    rows = kept_ref.shape[0] // cuts
    copies = []
    for i, (source, to) in enumerate(((taken_ref, 1 - slot), (kept_ref, slot))):
        for cut in range(cuts):
            part = pl.ds(cut * rows, rows)
            copies.append(pltpu.make_async_copy(source.at[part], out_ref.at[to, part], sems.at[i, cut]))
    for copy in copies:
        copy.start()
    for copy in copies:
        copy.wait()


def place(band, kept, taken):
    return pl.pallas_call(
        place_kernel,
        out_shape=jax.ShapeDtypeStruct((MOST,) + kept.shape, kept.dtype),
        in_specs=[IN_SMEM, IN_VMEM, IN_VMEM],
        out_specs=IN_HBM,
        scratch_shapes=[pltpu.SemaphoreType.DMA((MOST, 4))],
        compiler_params=PARAMS,
        name="place",
    )(band, kept, taken)


def on_device(grads, owner):
    local_grads = grads[0]
    block_count, extent, columns = local_grads.shape
    devices = Z * Y * CORE
    core = lax.axis_index("core").reshape(1).astype(jnp.int32)
    y = lax.axis_index("y").reshape(1).astype(jnp.int32)
    z = lax.axis_index("z").reshape(1).astype(jnp.int32)
    band = lax.axis_index("mp").reshape(1).astype(jnp.int32)
    chosen = selection(owner, core, block_count, extent // devices)

    def swap(value):
        return lax.ppermute(value, "core", [(0, 1), (1, 0)])

    def up(value):
        return lax.ppermute(value, "y", [(i, (i + 1) % Y) for i in range(Y)])

    def down(value):
        return lax.ppermute(value, "y", [(i, (i - 1) % Y) for i in range(Y)])

    def along(value, to):
        return lax.ppermute(value, "mp", list(enumerate(to)))

    n = block_count // 2
    sent = pieces_of(local_grads, core, y, [(True, shift) for shift in (2, 1, 3)], "sent")
    far, near_up, near_down = (swap(piece) for piece in sent)
    kept_far, kept_up, kept_down = pieces_of(local_grads, core, y, [(False, shift) for shift in (2, 1, 3)], "kept")
    v2a, v2b = add_parts(
        [[(0, 0, 0, n), (1, 0, 0, n)], [(0, 0, n, n), (1, 0, n, n)]], (kept_far, far), jnp.bfloat16, "far_sum"
    )
    from_down, from_up = up(v2a), down(v2b)
    (v1b,) = add_parts([[(0, 0, n, n), (1, 0, n, n)]], (kept_up, near_up), jnp.bfloat16, "near_up")
    (v3a,) = add_parts([[(0, 0, 0, n), (1, 0, 0, n)]], (kept_down, near_down), jnp.bfloat16, "near_down")
    v_up, v_down = up(v1b), down(v3a)
    kept_up, kept_down, v1b, v3a, own_grads = lax.optimization_barrier(
        (kept_up, kept_down, v1b, v3a, local_grads)
    )
    (sent_own,) = pieces_of(own_grads, core, y, [(True, 0)], "own_piece")
    own = swap(sent_own)
    (w1a,) = add_parts(
        [[(0, 0, 0, n), (1, 0, 0, n), (2, 0, 0, n)]], (kept_up, near_up, from_down), jnp.bfloat16, "relay_up"
    )
    (w3b,) = add_parts(
        [[(0, 0, n, n), (1, 0, n, n), (2, 0, 0, n)]], (kept_down, near_down, from_up), jnp.bfloat16, "relay_down"
    )
    w_up, w_down = up(w1a), down(w3b)
    own_a, own_b = own_sum(local_grads, core, y, own, v_up, v_down)
    own_a, own_b, chosen, band = lax.optimization_barrier((own_a, own_b, chosen, band))
    sent_a, sent_b, kept = plane_sum(z, own_a, own_b, w_down, w_up)
    got_a = lax.ppermute(sent_a, "z", [(i, i ^ 1) for i in range(Z)])
    got_b = lax.ppermute(sent_b, "z", [(i, (i - 1 + 2 * (i % 2)) % Z) for i in range(Z)])
    *sent, own = parity_sum(z, kept, got_a, got_b)
    received = [
        lax.ppermute(value, "z", [(i, i ^ change) for i in range(Z)]) for value, change in zip(sent, (4, 6, 2))
    ]
    mine = mean_rows(own, received, devices)

    outgoing = select(core, chosen, mine, swap(mine)).reshape(Z * Y, MOST, -1, columns)
    arrived = lax.all_to_all(outgoing, ("z", "y"), split_axis=0, concat_axis=0, tiled=True)
    own_band, next_band = bands_of(band, arrived)
    outer = along(next_band, (3, 2, 1, 0))
    same = along(own_band, (2, 3, 0, 1))
    partner = along(next_band, (1, 0, 3, 2))

    result = pltpu.VMEM((extent, columns), jnp.bfloat16)
    kept, given = pl.pallas_call(
        precondition_kernel,
        out_shape=(result, result),
        in_specs=[IN_VMEM] * MP,
        out_specs=[IN_VMEM] * 2,
        compiler_params=LARGE,
        name="precondition",
    )(same, outer, partner, own_band)
    return place(band, kept, along(given, (1, 0, 3, 2)))


def solution(mesh):
    split = Mesh(mesh.devices.reshape(Z, Y, CORE, MP), ("z", "y", "core", "mp"))
    placed = (P(DP, None, None, "mp"), P())
    return jax.shard_map(
        on_device, mesh=split, in_specs=placed, out_specs=P(DP, None, "mp"), check_vma=False
    )
```
